32 devices in a mesh: age: 8 (over y, x, core), box: 4 (over z).
Axes of the slice: x: 2, y: 2, z: 4, core: 2. Of those that a mesh axis runs over, the one named last changes fastest.
Arguments:
- position: float32 [3, 131072], P(None, ('age', 'box')), may hold values from -6 to 6
- strength: float32 [3, 131072], P(None, ('age', 'box')), may hold values from -6 to 6
- node_box: int32 [131072], P(('age', 'box')), may hold values from 0 to 1023, as said below
- box_order: int32 [1024], P(('age', 'box')), may hold values from 0 to 1023, as said below
- box_center: float32 [3, 1024], P(None, ('age', 'box')), may hold values from -6 to 6
- near_list: int32 [1024, 4], P(('age', 'box')), may hold values from -1 to 1023, as said below
- m2l_source: int32 [1024, 32], P(('age', 'box')), may hold values from 0 to 1023
- m2l_type: int32 [1024, 32], P(('age', 'box')), may hold values from 0 to 15
- basis_dir: float32 [3, 256], replicated, may hold values from -3.5 to 3.5
- basis_freq: float32 [3, 256], replicated, may hold values from -6 to 6
- basis_phase: float32 [256], replicated, may hold values from -3.140625 to 3.140625
- translation: bfloat16 [16, 256, 256], replicated, may hold values from -0.0012207031 to 0.0012207031
Outputs:
- velocity: float32 [3, 131072], P(None, ('age', 'box'))
The draws below stay inside these ranges and needn't reach their ends.
Inputs may be any that keep to these rules, and one draw needn't show every extreme that they name: box_order is a permutation of the box ids. `node_box`: every entry is a box id. Of the 4096 nodes of one device (aligned blocks of 4096 entries), at most 256 lie in the boxes held by any one device, that is the boxes box_order[g * 32] to box_order[g * 32 + 31]; in every draw some device holds the boxes of exactly 256 nodes of every device. Over all nodes, at most 256 lie in any one box, and in every draw some box holds exactly 256. `near_list`: row p lists box_order[p] first, then distinct other boxes held by the same device as position p, then -1 padding. `m2l_source`: entries are box ids; repeats may occur.
All inputs are finite; a program needn't handle non-finite values.
Results may differ from the reference program's by a relative error of at most 0.0025.
Values may be sent and summed in bfloat16 or wider, within the bound.
A program may use at most 64 MiB of HBM per device.

```python
import jax
import jax.numpy as jnp
from jax import lax

NODE_DEV = 4096
BOX_DEV = 32
COEF = 256
TYPES = 16
LIST = 32
NEAR = 4
GROUPS = 32
CAP = 256
NODES = 131072
BOXES = 1024
N_AGE = 8
N_BOX = 4


def owner_order(key):
    return jax.random.permutation(jax.random.fold_in(key, 11), BOXES).astype(jnp.int32)


def draw_box_order(key, part):
    return owner_order(key)


def draw_node_box(key, part):
    order_table = owner_order(key)
    hottest = jax.random.randint(jax.random.fold_in(key, 12), (), 0, GROUPS).astype(jnp.int32)
    label_count = (GROUPS - 1) * CAP
    group_ids = jnp.arange(GROUPS, dtype=jnp.int32)

    def one_source(source_key):
        picks = jax.random.permutation(jax.random.fold_in(source_key, 1), label_count)[:NODE_DEV - CAP]
        target = (picks // CAP).astype(jnp.int32)
        target = target + (target >= hottest).astype(jnp.int32)
        target = jnp.concatenate([jnp.full((CAP,), 1, jnp.int32) * hottest, target])
        target = jax.random.permutation(jax.random.fold_in(source_key, 2), target)
        target_hits = (target[:, None] == group_ids[None, :]).astype(jnp.int32)
        rank_in = jnp.sum(jnp.cumsum(target_hits, axis=0) * target_hits, axis=1) - 1
        rotation = jax.random.randint(jax.random.fold_in(source_key, 3), (GROUPS,), 0, BOX_DEV).astype(jnp.int32)
        within = ((rank_in + rotation[target]) % BOX_DEV).astype(jnp.int32)
        return order_table[target * BOX_DEV + within]
    source_keys = jax.random.split(jax.random.fold_in(key, 13), GROUPS)
    return jax.vmap(one_source)(source_keys).reshape(-1).astype(jnp.int32)


def draw_near_list(key, part):
    order_table = owner_order(key)
    row_ids = jnp.arange(BOXES, dtype=jnp.int32)
    local_idx = row_ids % BOX_DEV
    base_row = row_ids - local_idx

    def one_row(row_key):
        return jax.random.permutation(row_key, BOX_DEV - 1)[:NEAR - 1].astype(jnp.int32)
    picks = jax.vmap(one_row)(jax.random.split(jax.random.fold_in(key, 14), BOXES))
    others = base_row[:, None] + (local_idx[:, None] + 1 + picks) % BOX_DEV
    kept = jax.random.randint(jax.random.fold_in(key, 15), (BOXES,), 1, NEAR + 1).astype(jnp.int32)
    kept = jnp.where(local_idx == 0, NEAR, jnp.where(local_idx == 1, 1, kept))
    entries = jnp.concatenate([row_ids[:, None], others], axis=1)
    keep_flag = jnp.arange(NEAR, dtype=jnp.int32)[None, :] < kept[:, None]
    return jnp.where(keep_flag, order_table[entries], -1).astype(jnp.int32)


def place_ends(values, rng, low, largest):
    longest = values.shape.index(max(values.shape))
    spots = []
    for shift in (0, 1):
        where = [jax.random.randint(jax.random.fold_in(rng, axis), (), 0, length) for axis, length in enumerate(values.shape)]
        where[longest] = (where[longest] + shift) % values.shape[longest]
        spots.append(tuple(where))
    return values.at[spots[0]].set(low).at[spots[1]].set(largest)


def block_scale(stream_key, shape, cuts, smallest, top_value):
    def one(dim, parts):
        draws = jax.random.uniform(jax.random.fold_in(jax.random.fold_in(stream_key, 6), dim), (parts,), jnp.float32, smallest / len(cuts), top_value / len(cuts))
        return jnp.repeat(jnp.exp(draws), shape[dim] // parts).reshape((-1,) + (1,) * (len(shape) - dim - 1))

    loudness = one(*cuts[0])
    for cut in cuts[1:]:
        loudness = loudness * one(*cut)
    return loudness


def bell_draw(rng, shape, scale, reach, cuts=(), kind=jnp.bfloat16):
    drawn = scale * jax.random.normal(rng, shape, jnp.float32)
    if cuts:
        drawn = drawn * block_scale(rng, shape, cuts, -0.22, 0.18)
    return jnp.clip(drawn, -reach, reach).astype(kind)


def setup_inputs(seed: int = 0) -> dict:
    key_list = jax.random.split(jax.random.key(seed), 13)
    return {
        "position": bell_draw(key_list[0], (3, NODES), 1.0, 6.0, ((1, 32),), jnp.float32),
        "strength": bell_draw(key_list[1], (3, NODES), 1.0, 6.0, ((1, 32),), jnp.float32),
        "node_box": draw_node_box(jax.random.fold_in(key_list[12], 71), 0),
        "box_order": draw_box_order(jax.random.fold_in(key_list[12], 71), 0),
        "box_center": bell_draw(key_list[4], (3, BOXES), 1.0, 6.0, ((1, 32),), jnp.float32),
        "near_list": draw_near_list(jax.random.fold_in(key_list[12], 71), 0),
        "m2l_source": place_ends(jax.random.randint(key_list[6], (BOXES, LIST), 0, BOXES), jax.random.fold_in(key_list[6], 1), 0, BOXES - 1).astype(jnp.int32),
        "m2l_type": place_ends(jax.random.randint(key_list[7], (BOXES, LIST), 0, TYPES), jax.random.fold_in(key_list[7], 1), 0, TYPES - 1).astype(jnp.int32),
        "basis_dir": bell_draw(key_list[8], (3, COEF), 3 ** -0.5, 3.5, (), jnp.float32),
        "basis_freq": bell_draw(key_list[9], (3, COEF), 1.5, 6.0, (), jnp.float32),
        "basis_phase": jnp.clip(jax.random.uniform(key_list[10], (COEF,), jnp.float32, -3.140625, 3.140625), -3.140625, 3.140625),
        "translation": bell_draw(key_list[11], (TYPES, COEF, COEF), (20 * COEF * LIST * NODE_DEV // BOX_DEV) ** -0.5, 0.0012207031),
    }


core_square = 0.01
inv_four_pi = 0.07957747154594767

def expansion(offsets, charges, basis_dir, basis_freq, basis_phase):
    phase_arg = basis_freq[0][:, None] * offsets[0][None, :] + basis_freq[1][:, None] * offsets[1][None, :] + basis_freq[2][:, None] * offsets[2][None, :] + basis_phase[:, None]
    wave_vals = jnp.cos(phase_arg)
    weight = basis_dir[0][:, None] * charges[0][None, :] + basis_dir[1][:, None] * charges[1][None, :] + basis_dir[2][:, None] * charges[2][None, :]
    return (wave_vals, weight)

def near_field(target_pos, source_pos, source_str, pair_mask):
    delta_x = target_pos[0][:, None] - source_pos[0][None, :]
    delta_y = target_pos[1][:, None] - source_pos[1][None, :]
    delta_z = target_pos[2][:, None] - source_pos[2][None, :]
    distance = delta_x * delta_x + delta_y * delta_y + delta_z * delta_z + core_square
    factor = pair_mask * inv_four_pi / (distance * jnp.sqrt(distance))
    vel_x = lax.optimization_barrier(jnp.sum(factor * (source_str[1][None, :] * delta_z - source_str[2][None, :] * delta_y), axis=1))
    vel_y = lax.optimization_barrier(jnp.sum(factor * (source_str[2][None, :] * delta_x - source_str[0][None, :] * delta_z), axis=1))
    vel_z = lax.optimization_barrier(jnp.sum(factor * (source_str[0][None, :] * delta_y - source_str[1][None, :] * delta_x), axis=1))
    return jnp.stack([vel_x, vel_y, vel_z])

def near_blocks(slot_pos, slot_str, member, reach_map):
    slots_total = slot_pos.shape[1]
    block_rows = min(512, slots_total)
    block_count = slots_total // block_rows
    target_pos = slot_pos.reshape(3, block_count, block_rows).transpose(1, 0, 2)
    target_hits = member.reshape(member.shape[0], block_count, block_rows).transpose(1, 0, 2)

    def one_block(block_args):
        block_pos, block_hits = block_args
        pair_mask = lax.dot_general(block_hits, reach_map, (((0,), (0,)), ((), ())), precision=lax.Precision.HIGHEST)
        return near_field(block_pos, slot_pos, slot_str, pair_mask)
    result = lax.map(one_block, (target_pos, target_hits))
    return result.transpose(1, 0, 2).reshape(3, slots_total)

def reference(position, strength, node_box, box_order, box_center, near_list, m2l_source, m2l_type, basis_dir, basis_freq, basis_phase, translation):
    largest_level = lax.Precision.HIGHEST
    groups = N_AGE * N_BOX
    slots_total = 2 * NODE_DEV
    node_count = position.shape[1]
    slot_of_box = jnp.zeros((BOXES,), jnp.int32).at[box_order].set(jnp.arange(BOXES, dtype=jnp.int32))
    node_slot = slot_of_box[node_box]
    owner = (node_slot // BOX_DEV).astype(jnp.int32)
    sorted_idx = jnp.argsort(owner, stable=True).astype(jnp.int32)
    sorted_owner = owner[sorted_idx]
    group_sizes = jnp.zeros((groups,), jnp.int32).at[owner].add(1)
    group_starts = (jnp.cumsum(group_sizes) - group_sizes).astype(jnp.int32)
    rank_within = (jnp.arange(node_count, dtype=jnp.int32) - group_starts[sorted_owner]).astype(jnp.int32)
    slot_table = jnp.full((groups, slots_total), node_count, jnp.int32).at[sorted_owner, rank_within].set(sorted_idx)
    pos_pad = jnp.concatenate([position, jnp.zeros((3, 1), jnp.float32)], axis=1)
    str_pad = jnp.concatenate([strength, jnp.zeros((3, 1), jnp.float32)], axis=1)
    box_pad = jnp.concatenate([node_box, jnp.full((1,), -1, jnp.int32)])

    def group_inputs(group_idx):
        node_index = slot_table[group_idx]
        slot_pos = pos_pad[:, node_index]
        slot_str = str_pad[:, node_index]
        slot_box = box_pad[node_index]
        first_box = (group_idx * BOX_DEV).astype(jnp.int32)
        local_ids = lax.dynamic_slice_in_dim(box_order, first_box, BOX_DEV)
        member = (slot_box[None, :] == local_ids[:, None]).astype(jnp.float32)
        centers = lax.dynamic_slice_in_dim(box_center, first_box, BOX_DEV, 1)
        offsets = slot_pos - jnp.dot(centers, member, precision=largest_level)
        wave_vals, weight = expansion(offsets, slot_str, basis_dir, basis_freq, basis_phase)
        return (slot_pos, slot_str, local_ids, member, wave_vals, weight)

    def group_blocks(group_idx):
        slot_pos, slot_str, local_ids, member, wave_vals, weight = group_inputs(group_idx)
        return lax.dot_general(member, wave_vals * weight, (((1,), (1,)), ((), ())), precision=largest_level)
    blocks = lax.map(group_blocks, jnp.arange(groups, dtype=jnp.int32)).reshape(BOXES, COEF).astype(jnp.bfloat16)
    source_slot = slot_of_box[m2l_source]
    picked = blocks[source_slot].astype(jnp.float32)
    kind_hits = (m2l_type[:, :, None] == jnp.arange(TYPES, dtype=jnp.int32)[None, None, :]).astype(jnp.float32)
    mixed_blocks = jnp.einsum('plt,plc->ptc', kind_hits, picked, precision=largest_level).astype(jnp.bfloat16)
    expansions = jnp.einsum('ptc,tkc->pk', mixed_blocks.astype(jnp.float32), translation.astype(jnp.float32), precision=largest_level)

    def group_velocity(group_idx):
        slot_pos, slot_str, local_ids, member, wave_vals, weight = group_inputs(group_idx)
        first_box = (group_idx * BOX_DEV).astype(jnp.int32)
        near_rows = lax.dynamic_slice_in_dim(near_list, first_box, BOX_DEV, 0)
        allowed = jnp.any(near_rows[:, :, None] == local_ids[None, None, :], axis=1).astype(jnp.float32)
        reach_map = jnp.dot(allowed, member, precision=largest_level)
        near_vel = near_blocks(slot_pos, slot_str, member, reach_map)
        group_exp = lax.dynamic_slice_in_dim(expansions, first_box, BOX_DEV, 0)
        slot_position_here = jnp.dot(group_exp.T, member, precision=largest_level)
        far_vel = jnp.dot(basis_dir, wave_vals * slot_position_here, precision=largest_level)
        return near_vel + far_vel
    velocities = lax.map(group_velocity, jnp.arange(groups, dtype=jnp.int32))
    spread = velocities.transpose(1, 0, 2).reshape(3, groups * slots_total)
    result = jnp.zeros((3, node_count + 1), jnp.float32).at[:, slot_table.reshape(-1)].set(spread)
    return result[:, :node_count]
```

```python
import functools

import jax
import jax.numpy as jnp
import numpy as np
from jax import lax
from jax.experimental import pallas as pl
from jax.experimental.pallas import tpu as pltpu
from jax.sharding import PartitionSpec as P

AXES = ("age", "box")
core_square = 0.01
inv_four_pi = 0.07957747154594767
inv_two_pi = 0.15915494309189535
LANES = 128
VMEM_LIMIT = 48 * 1024 * 1024


def cos_coefficients(degree):
    nodes = np.cos(np.pi * (np.arange(64) + 0.5) / 64)
    w = 0.125 * (nodes + 1.0)
    fit = np.polynomial.chebyshev.Chebyshev.fit(
        w, np.cos(2 * np.pi * np.sqrt(w)), degree, domain=[0, 0.25]
    )
    return [float(c) for c in fit.convert(kind=np.polynomial.Polynomial).coef]


COS_COEF = cos_coefficients(8)


def cos_turns(turns):
    v = turns - jnp.round(turns)
    w = v * v
    acc = jnp.full_like(w, COS_COEF[-1])
    for c in COS_COEF[-2::-1]:
        acc = acc * w + c
    return acc


def gather_body(n_box, n, x_ref, o_ref, send_sem, recv_sem):
    me = lax.axis_index("age") * n_box + lax.axis_index("box")
    barrier = pltpu.get_barrier_semaphore()

    def peer(d):
        other = lax.rem(me + d, n)
        return {"age": other // n_box, "box": lax.rem(other, n_box)}

    def greet(d, carry):
        pl.semaphore_signal(
            barrier, inc=1, device_id=peer(d), device_id_type=pl.DeviceIdType.MESH
        )
        return carry

    lax.fori_loop(1, n, greet, 0)
    o_ref[me] = x_ref[...]
    pl.semaphore_wait(barrier, n - 1)

    def copy(d):
        return pltpu.make_async_remote_copy(
            src_ref=x_ref,
            dst_ref=o_ref.at[me],
            send_sem=send_sem.at[d - 1],
            recv_sem=recv_sem.at[d - 1],
            device_id=peer(d),
            device_id_type=pl.DeviceIdType.MESH,
        )

    def send(d, carry):
        copy(d).start()
        return carry

    def finish(d, carry):
        copy(d).wait()
        return carry

    lax.fori_loop(1, n, send, 0)
    lax.fori_loop(1, n, finish, 0)


def gather_blocks(x, n_box, n, collective_id):
    return pl.pallas_call(
        functools.partial(gather_body, n_box, n),
        out_shape=jax.ShapeDtypeStruct((n,) + x.shape, x.dtype),
        in_specs=[pl.BlockSpec(memory_space=pltpu.VMEM)],
        out_specs=pl.BlockSpec(memory_space=pltpu.VMEM),
        scratch_shapes=[
            pltpu.SemaphoreType.DMA((n - 1,)),
            pltpu.SemaphoreType.DMA((n - 1,)),
        ],
        compiler_params=pltpu.CompilerParams(
            collective_id=collective_id, has_side_effects=True
        ),
    )(x)


def lanes_to_rows(tile):
    padded = jnp.concatenate([tile, jnp.zeros((LANES - tile.shape[0], LANES), tile.dtype)], axis=0)
    return padded.T


def fill_rows(src_ref, rows_ref, count):
    def step(i, carry):
        at = pl.multiple_of(i * LANES, LANES)
        rows_ref[pl.ds(at, LANES), :] = lanes_to_rows(src_ref[:, pl.ds(at, LANES)])
        return carry

    lax.fori_loop(0, count // LANES, step, 0)


def take_lanes(rows_ref, out_ref, count):
    def step(i, carry):
        at = pl.multiple_of(i * LANES, LANES)
        out_ref[:, pl.ds(at, LANES)] = rows_ref[pl.ds(at, LANES), :].T[: out_ref.shape[0]]
        return carry

    lax.fori_loop(0, count // LANES, step, 0)


def zero_rows(ref):
    def step(i, carry):
        at = pl.multiple_of(i * 8, 8)
        ref[pl.ds(at, 8), :] = jnp.zeros((8, LANES), jnp.float32)
        return carry

    lax.fori_loop(0, ref.shape[0] // 8, step, 0, unroll=8)


def scatter_rows(idx_ref, src_ref, dst_ref, count):
    def step(i, carry):
        at = pl.multiple_of(i * 16, 16)
        block = src_ref[pl.ds(at, 16), :]
        for u in range(16):
            dst_ref[pl.ds(idx_ref[at + u], 1), :] = block[u : u + 1, :]
        return carry

    lax.fori_loop(0, count // 16, step, 0)


def gather_rows(idx_ref, src_ref, dst_ref, count):
    def step(i, carry):
        at = pl.multiple_of(i * 16, 16)
        rows = [src_ref[pl.ds(idx_ref[at + u], 1), :] for u in range(16)]
        dst_ref[pl.ds(at, 16), :] = jnp.concatenate(rows, axis=0)
        return carry

    lax.fori_loop(0, count // 16, step, 0)


def spread_body(idx_ref, x_ref, out_ref, rows, placed):
    fill_rows(x_ref, rows, x_ref.shape[1])
    zero_rows(placed)
    scatter_rows(idx_ref, rows, placed, x_ref.shape[1])
    take_lanes(placed, out_ref, out_ref.shape[1])


def group_body(idx_ref, x_ref, out_ref, rows):
    fill_rows(x_ref, rows, x_ref.shape[1])
    zero_rows(out_ref)
    scatter_rows(idx_ref, rows, out_ref, x_ref.shape[1])


def ungroup_body(idx_ref, x_ref, out_ref, rows):
    gather_rows(idx_ref, x_ref, rows, out_ref.shape[1])
    take_lanes(rows, out_ref, out_ref.shape[1])


def collect_body(idx_ref, x_ref, out_ref, src, rows):
    fill_rows(x_ref, src, x_ref.shape[1])
    gather_rows(idx_ref, src, rows, out_ref.shape[1])
    take_lanes(rows, out_ref, out_ref.shape[1])


def permute_call(body, idx, x, out_shape, scratch_rows):
    return pl.pallas_call(
        body,
        out_shape=jax.ShapeDtypeStruct(out_shape, jnp.float32),
        in_specs=[
            pl.BlockSpec(memory_space=pltpu.SMEM),
            pl.BlockSpec(memory_space=pltpu.VMEM),
        ],
        out_specs=pl.BlockSpec(memory_space=pltpu.VMEM),
        scratch_shapes=[pltpu.VMEM((r, LANES), jnp.float32) for r in scratch_rows],
        compiler_params=pltpu.CompilerParams(vmem_limit_bytes=VMEM_LIMIT),
    )(idx, x)


def ranks(key, kinds):
    count = key.shape[0]
    blocks = count // LANES
    hits = (key[None, :] == jnp.arange(kinds, dtype=jnp.int32)[:, None]).reshape(
        kinds, blocks, LANES
    )
    hits16 = hits.astype(jnp.bfloat16)
    lane = np.arange(LANES)
    before = jnp.asarray(lane[:, None] < lane[None, :], jnp.bfloat16)
    inside = jnp.dot(
        hits16.reshape(kinds * blocks, LANES), before, preferred_element_type=jnp.float32
    ).reshape(kinds, blocks, LANES)
    totals = jnp.sum(hits.astype(jnp.float32), axis=2)
    block = np.arange(blocks)
    base = jnp.dot(
        totals.astype(jnp.bfloat16),
        jnp.asarray(block[:, None] < block[None, :], jnp.bfloat16),
        preferred_element_type=jnp.float32,
    )
    rank = jnp.sum(jnp.where(hits, inside + base[:, :, None], 0.0), axis=0)
    return rank.reshape(count).astype(jnp.int32)


def split16(x):
    high = x.astype(jnp.bfloat16)
    return high, (x - high.astype(jnp.float32)).astype(jnp.bfloat16)


def box_body(center_ref, rows_ref, basis_ref, block_ref, wave_ref, lanes_ref, parts_ref):
    b = pl.program_id(0)
    count = rows_ref.shape[0]
    cx, cy, cz = center_ref[0, b], center_ref[1, b], center_ref[2, b]
    fx, fy, fz = basis_ref[0:1, :], basis_ref[1:2, :], basis_ref[2:3, :]
    phase = basis_ref[3:4, :]
    ux, uy, uz = basis_ref[4:5, :], basis_ref[5:6, :], basis_ref[6:7, :]
    chunk = 32
    total = jnp.zeros((8, fx.shape[1]), jnp.float32)
    for c in range(count // chunk):
        r = rows_ref[c * chunk : (c + 1) * chunk, :]
        turns = (
            fx * (r[:, 0:1] - cx) + fy * (r[:, 1:2] - cy) + fz * (r[:, 2:3] - cz) + phase
        )
        wave = cos_turns(turns)
        wave_ref[c * chunk : (c + 1) * chunk, :] = wave
        charge = ux * r[:, 3:4] + uy * r[:, 4:5] + uz * r[:, 5:6]
        product = charge * wave
        for s in range(chunk // 8):
            total = total + product[s * 8 : (s + 1) * 8]
    block_ref[0] = jnp.sum(total, axis=0, keepdims=True)
    lanes = jnp.concatenate(
        [rows_ref[i * LANES : (i + 1) * LANES, :].T[:8] for i in range(count // LANES)], axis=1
    )
    lanes_ref[0] = lanes
    x, y, z = lanes[0:1], lanes[1:2], lanes[2:3]
    sx, sy, sz = lanes[3:4], lanes[4:5], lanes[5:6]
    zero = jnp.zeros_like(x)
    table = jnp.concatenate(
        [sx, sy, sz, zero, sy * z - sz * y, sz * x - sx * z, sx * y - sy * x, zero], axis=0
    )
    high = table.astype(jnp.bfloat16).astype(jnp.float32)
    parts_ref[0] = jnp.concatenate([high, table - high], axis=0).astype(jnp.bfloat16)


def box_call(center, rows, basis, boxes, per_box):
    coef = basis.shape[1]
    return pl.pallas_call(
        box_body,
        grid=(boxes,),
        out_shape=(
            jax.ShapeDtypeStruct((boxes, 1, coef), jnp.float32),
            jax.ShapeDtypeStruct((boxes * per_box, coef), jnp.float32),
            jax.ShapeDtypeStruct((boxes, 8, per_box), jnp.float32),
            jax.ShapeDtypeStruct((boxes, 16, per_box), jnp.bfloat16),
        ),
        in_specs=[
            pl.BlockSpec(memory_space=pltpu.SMEM),
            pl.BlockSpec((per_box, LANES), lambda b: (b, 0)),
            pl.BlockSpec((8, coef), lambda b: (0, 0)),
        ],
        out_specs=(
            pl.BlockSpec((1, 1, coef), lambda b: (b, 0, 0)),
            pl.BlockSpec((per_box, coef), lambda b: (b, 0)),
            pl.BlockSpec((1, 8, per_box), lambda b: (b, 0, 0)),
            pl.BlockSpec((1, 16, per_box), lambda b: (b, 0, 0)),
        ),
        compiler_params=pltpu.CompilerParams(vmem_limit_bytes=VMEM_LIMIT),
    )(center, rows, basis)


def velocity_body(
    near_ref, rows_ref, lanes_ref, parts_ref, wave_ref, exp_ref, dir_ref, out_ref, acc
):
    b = pl.program_id(0)
    per_box = wave_ref.shape[0]
    lanes = lanes_ref[b]
    tx, ty, tz = lanes[0:1], lanes[1:2], lanes[2:3]
    acc[...] = jnp.zeros_like(acc)
    chunk = 64
    for v in range(near_ref.shape[1]):
        j = near_ref[b, v]

        @pl.when(j >= 0)
        def _():
            start = j * per_box
            pieces = []
            for c in range(per_box // chunk):
                at = pl.multiple_of(start + c * chunk, chunk)
                s = rows_ref[pl.ds(at, chunk), :]
                dx = tx - s[:, 0:1]
                dy = ty - s[:, 1:2]
                dz = tz - s[:, 2:3]
                r = lax.rsqrt(dx * dx + dy * dy + dz * dz + core_square)
                pieces.append((r * r * r).astype(jnp.bfloat16))
            factor = jnp.concatenate(pieces, axis=0)
            acc[...] += jnp.dot(parts_ref[j], factor, preferred_element_type=jnp.float32)

    sums = acc[...]
    sums = sums[0:8] + sums[8:16]
    ax, ay, az = sums[0:1], sums[1:2], sums[2:3]
    nx = ay * tz - az * ty - sums[4:5]
    ny = az * tx - ax * tz - sums[5:6]
    nz = ax * ty - ay * tx - sums[6:7]
    near = jnp.concatenate([nx, ny, nz, jnp.zeros((5, per_box), jnp.float32)], axis=0)
    near = near * inv_four_pi
    high, low = split16(wave_ref[...] * exp_ref[0])
    table = dir_ref[...]
    both = jnp.dot(high, table, preferred_element_type=jnp.float32)
    both = both + jnp.dot(low, table, preferred_element_type=jnp.float32)
    far = both[:, :LANES] + both[:, LANES:]
    for i in range(per_box // LANES):
        out_ref[i * LANES : (i + 1) * LANES, :] = far[
            i * LANES : (i + 1) * LANES
        ] + lanes_to_rows(near[:, i * LANES : (i + 1) * LANES])


def velocity_call(near, rows, lanes, parts, wave, exps, table, boxes, per_box):
    coef = wave.shape[1]
    return pl.pallas_call(
        velocity_body,
        grid=(boxes,),
        out_shape=jax.ShapeDtypeStruct((boxes * per_box, LANES), jnp.float32),
        in_specs=[
            pl.BlockSpec(memory_space=pltpu.SMEM),
            pl.BlockSpec(memory_space=pltpu.VMEM),
            pl.BlockSpec(memory_space=pltpu.VMEM),
            pl.BlockSpec(memory_space=pltpu.VMEM),
            pl.BlockSpec((per_box, coef), lambda b: (b, 0)),
            pl.BlockSpec((1, 1, coef), lambda b: (b, 0, 0)),
            pl.BlockSpec(memory_space=pltpu.VMEM),
        ],
        out_specs=pl.BlockSpec((per_box, LANES), lambda b: (b, 0)),
        scratch_shapes=[pltpu.VMEM((16, per_box), jnp.float32)],
        compiler_params=pltpu.CompilerParams(vmem_limit_bytes=VMEM_LIMIT),
    )(near, rows, lanes, parts, wave, exps, table)


def per_device(
    n_box,
    groups,
    position,
    strength,
    node_box,
    box_order,
    box_center,
    near_list,
    m2l_source,
    m2l_type,
    basis_dir,
    basis_freq,
    basis_phase,
    translation,
):
    node_count = position.shape[1]
    box_local = box_order.shape[0]
    slots_total = 2 * node_count
    per_peer = slots_total // groups
    per_box = slots_total // box_local
    coef = basis_phase.shape[0]
    kind_count = translation.shape[0]
    box_total = groups * box_local

    padded_order = jnp.pad(box_order, (0, LANES - box_local)).reshape(1, LANES)
    all_order = gather_blocks(padded_order, n_box, groups, 0)[:, 0, :box_local].reshape(-1)

    node_slot = jnp.sum(
        jnp.where(
            node_box[None, :] == all_order[:, None],
            jnp.arange(box_total, dtype=jnp.int32)[:, None],
            0,
        ),
        axis=0,
    )
    owner = node_slot // box_local
    label = (node_slot - owner * box_local + 1).astype(jnp.float32)
    send_at = owner * per_peer + ranks(owner, groups)
    fields = jnp.concatenate(
        [position, strength, label[None, :], jnp.zeros((1, node_count), jnp.float32)], axis=0
    )
    payload = permute_call(
        spread_body, send_at, fields, (8, slots_total), (node_count, slots_total)
    )
    got = lax.all_to_all(payload, AXES, split_axis=1, concat_axis=1, tiled=True)

    hit_source = (m2l_source[:, :, None] == all_order[None, None, :]).astype(jnp.bfloat16)
    kind_hits = (
        m2l_type[:, :, None] == jnp.arange(kind_count, dtype=jnp.int32)[None, None, :]
    ).astype(jnp.bfloat16)
    list_counts = jnp.einsum(
        "jlt,jlb->tjb", kind_hits, hit_source, preferred_element_type=jnp.float32
    )
    list_counts = list_counts.astype(jnp.bfloat16).reshape(kind_count * box_local, box_total)
    near_local = jnp.sum(
        jnp.where(
            near_list[:, :, None] == box_order[None, None, :],
            jnp.arange(1, box_local + 1, dtype=jnp.int32)[None, None, :],
            0,
        ),
        axis=2,
    ) - 1

    got_label = got[6].astype(jnp.int32) - 1
    live = got_label >= 0
    tile_at = jnp.where(
        live, got_label * per_box + ranks(got_label, box_local), slots_total
    )
    rows = permute_call(group_body, tile_at, got, (slots_total + 8, LANES), (slots_total,))
    basis = jnp.concatenate(
        [
            basis_freq * inv_two_pi,
            basis_phase[None, :] * inv_two_pi,
            basis_dir,
            jnp.zeros((1, coef), jnp.float32),
        ],
        axis=0,
    )
    sums, wave, lanes, parts = box_call(box_center, rows, basis, box_local, per_box)
    local_blocks = sums.reshape(box_local, coef).astype(jnp.bfloat16)
    all_blocks = gather_blocks(local_blocks, n_box, groups, 1).reshape(box_total, coef)
    mixed = jnp.dot(list_counts, all_blocks, preferred_element_type=jnp.float32)
    mixed = mixed.astype(jnp.bfloat16).reshape(kind_count, box_local, coef)
    expansions = jnp.einsum(
        "tjc,tkc->jk", mixed, translation, preferred_element_type=jnp.float32
    )
    dir_high, dir_low = split16(basis_dir.T)
    pad = ((0, 0), (0, LANES - 3))
    table = jnp.concatenate([jnp.pad(dir_high, pad), jnp.pad(dir_low, pad)], axis=1)
    vel_rows = velocity_call(
        near_local,
        rows,
        lanes,
        parts,
        wave,
        expansions.reshape(box_local, 1, coef),
        table,
        box_local,
        per_box,
    )
    back = permute_call(
        ungroup_body,
        jnp.minimum(tile_at, slots_total - 1),
        vel_rows,
        (8, slots_total),
        (slots_total,),
    )
    returned = lax.all_to_all(back[:3], AXES, split_axis=1, concat_axis=1, tiled=True)
    returned = jnp.pad(returned, ((0, 5), (0, 0)))
    out = permute_call(
        collect_body, send_at, returned, (8, node_count), (slots_total, node_count)
    )
    return out[:3]


def solution(mesh):
    n_box = mesh.shape["box"]
    groups = mesh.shape["age"] * n_box
    placed = (
        P(None, AXES),
        P(None, AXES),
        P(AXES),
        P(AXES),
        P(None, AXES),
        P(AXES, None),
        P(AXES, None),
        P(AXES, None),
        P(),
        P(),
        P(),
        P(),
    )
    return jax.shard_map(
        functools.partial(per_device, n_box, groups),
        mesh=mesh,
        in_specs=placed,
        out_specs=P(None, AXES),
        check_vma=False,
    )
```

```python
import functools

import jax
import jax.numpy as jnp
import numpy as np
from jax import lax
from jax.experimental import pallas as pl
from jax.experimental.pallas import tpu as pltpu
from jax.sharding import PartitionSpec as P

AXES = ("age", "box")
core_square = 0.01
inv_four_pi = 0.07957747154594767
inv_two_pi = 0.15915494309189535
LANES = 128
VMEM_LIMIT = 48 * 1024 * 1024


def cos_coefficients(degree):
    nodes = np.cos(np.pi * (np.arange(64) + 0.5) / 64)
    w = 0.125 * (nodes + 1.0)
    fit = np.polynomial.chebyshev.Chebyshev.fit(
        w, np.cos(2 * np.pi * np.sqrt(w)), degree, domain=[0, 0.25]
    )
    return [float(c) for c in fit.convert(kind=np.polynomial.Polynomial).coef]


COS_COEF = cos_coefficients(6)


def cos_turns(turns):
    v = turns - ((turns + 12582912.0) - 12582912.0)
    w = v * v
    acc = jnp.full_like(w, COS_COEF[-1])
    for c in COS_COEF[-2::-1]:
        acc = acc * w + c
    return acc


def gather_body(n_age, n_box, x_ref, o_ref, send_sem, recv_sem):
    me_age, me_box = lax.axis_index("age"), lax.axis_index("box")
    barrier = pltpu.get_barrier_semaphore()

    def on_box(d):
        return {"age": me_age, "box": lax.rem(me_box + d, n_box)}

    def on_age(d):
        return {"age": lax.rem(me_age + d, n_age), "box": me_box}

    def greet(peer):
        def step(d, carry):
            pl.semaphore_signal(
                barrier, inc=1, device_id=peer(d), device_id_type=pl.DeviceIdType.MESH
            )
            return carry

        return step

    lax.fori_loop(1, n_box, greet(on_box), 0)
    lax.fori_loop(1, n_age, greet(on_age), 0)
    o_ref[me_age, me_box] = x_ref[...]
    pl.semaphore_wait(barrier, n_box - 1 + n_age - 1)

    def along_box(d):
        return pltpu.make_async_remote_copy(
            src_ref=x_ref,
            dst_ref=o_ref.at[me_age, me_box],
            send_sem=send_sem.at[d - 1],
            recv_sem=recv_sem.at[d - 1],
            device_id=on_box(d),
            device_id_type=pl.DeviceIdType.MESH,
        )

    def along_age(d):
        return pltpu.make_async_remote_copy(
            src_ref=o_ref.at[me_age],
            dst_ref=o_ref.at[me_age],
            send_sem=send_sem.at[n_box - 2 + d],
            recv_sem=recv_sem.at[n_box - 2 + d],
            device_id=on_age(d),
            device_id_type=pl.DeviceIdType.MESH,
        )

    def start(copy):
        def step(d, carry):
            copy(d).start()
            return carry

        return step

    def finish(copy):
        def step(d, carry):
            copy(d).wait()
            return carry

        return step

    lax.fori_loop(1, n_box, start(along_box), 0)
    lax.fori_loop(1, n_box, finish(along_box), 0)
    lax.fori_loop(1, n_age, start(along_age), 0)
    lax.fori_loop(1, n_age, finish(along_age), 0)


def gather_blocks(x, n_age, n_box, collective_id):
    copies = n_age + n_box - 2
    return pl.pallas_call(
        functools.partial(gather_body, n_age, n_box),
        out_shape=jax.ShapeDtypeStruct((n_age, n_box) + x.shape, x.dtype),
        in_specs=[pl.BlockSpec(memory_space=pltpu.VMEM)],
        out_specs=pl.BlockSpec(memory_space=pltpu.VMEM),
        scratch_shapes=[
            pltpu.SemaphoreType.DMA((copies,)),
            pltpu.SemaphoreType.DMA((copies,)),
        ],
        compiler_params=pltpu.CompilerParams(
            collective_id=collective_id, has_side_effects=True
        ),
    )(x)


def lanes_to_rows(tile):
    padded = jnp.concatenate([tile, jnp.zeros((LANES - tile.shape[0], LANES), tile.dtype)], axis=0)
    return padded.T


def fill_rows(src_ref, rows_ref, count):
    def step(i, carry):
        at = pl.multiple_of(i * LANES, LANES)
        rows_ref[pl.ds(at, LANES), :] = lanes_to_rows(src_ref[:, pl.ds(at, LANES)])
        return carry

    lax.fori_loop(0, count // LANES, step, 0, unroll=8)


def take_lanes(rows_ref, out_ref, count):
    def step(i, carry):
        at = pl.multiple_of(i * LANES, LANES)
        out_ref[:, pl.ds(at, LANES)] = rows_ref[pl.ds(at, LANES), :].T[: out_ref.shape[0]]
        return carry

    lax.fori_loop(0, count // LANES, step, 0, unroll=8)


def zero_rows(ref):
    def step(i, carry):
        at = pl.multiple_of(i * 8, 8)
        ref[pl.ds(at, 8), :] = jnp.zeros((8, LANES), jnp.float32)
        return carry

    lax.fori_loop(0, ref.shape[0] // 8, step, 0, unroll=8)


def scatter_rows(idx_ref, src_ref, dst_ref, count):
    def step(i, carry):
        at = pl.multiple_of(i * 16, 16)
        block = src_ref[pl.ds(at, 16), :]
        for u in range(16):
            dst_ref[pl.ds(idx_ref[at + u], 1), :] = block[u : u + 1, :]
        return carry

    lax.fori_loop(0, count // 16, step, 0)


def gather_rows(idx_ref, src_ref, dst_ref, count):
    def step(i, carry):
        at = pl.multiple_of(i * 16, 16)
        rows = [src_ref[pl.ds(idx_ref[at + u], 1), :] for u in range(16)]
        dst_ref[pl.ds(at, 16), :] = jnp.concatenate(rows, axis=0)
        return carry

    lax.fori_loop(0, count // 16, step, 0)


def spread_body(idx_ref, x_ref, out_ref, rows, placed):
    fill_rows(x_ref, rows, x_ref.shape[1])
    zero_rows(placed)
    scatter_rows(idx_ref, rows, placed, x_ref.shape[1])
    take_lanes(placed, out_ref, out_ref.shape[1])


def group_body(idx_ref, x_ref, out_ref, rows):
    fill_rows(x_ref, rows, x_ref.shape[1])
    zero_rows(out_ref)
    scatter_rows(idx_ref, rows, out_ref, x_ref.shape[1])


def ungroup_body(idx_ref, x_ref, out_ref, rows):
    gather_rows(idx_ref, x_ref, rows, out_ref.shape[1])
    take_lanes(rows, out_ref, out_ref.shape[1])


def collect_body(idx_ref, x_ref, out_ref, src, rows):
    fill_rows(x_ref, src, x_ref.shape[1])
    gather_rows(idx_ref, src, rows, out_ref.shape[1])
    take_lanes(rows, out_ref, out_ref.shape[1])


def permute_call(body, idx, x, out_shape, scratch_rows):
    return pl.pallas_call(
        body,
        out_shape=jax.ShapeDtypeStruct(out_shape, jnp.float32),
        in_specs=[
            pl.BlockSpec(memory_space=pltpu.SMEM),
            pl.BlockSpec(memory_space=pltpu.VMEM),
        ],
        out_specs=pl.BlockSpec(memory_space=pltpu.VMEM),
        scratch_shapes=[pltpu.VMEM((r, LANES), jnp.float32) for r in scratch_rows],
        compiler_params=pltpu.CompilerParams(vmem_limit_bytes=VMEM_LIMIT),
    )(idx, x)


def ranks(key, kinds):
    count = key.shape[0]
    blocks = count // LANES
    hits = (key[None, :] == jnp.arange(kinds, dtype=jnp.int32)[:, None]).reshape(
        kinds, blocks, LANES
    )
    hits16 = hits.astype(jnp.bfloat16)
    lane = np.arange(LANES)
    before = jnp.asarray(lane[:, None] < lane[None, :], jnp.bfloat16)
    inside = jnp.dot(
        hits16.reshape(kinds * blocks, LANES), before, preferred_element_type=jnp.float32
    ).reshape(kinds, blocks, LANES)
    totals = jnp.sum(hits.astype(jnp.float32), axis=2)
    block = np.arange(blocks)
    base = jnp.dot(
        totals.astype(jnp.bfloat16),
        jnp.asarray(block[:, None] < block[None, :], jnp.bfloat16),
        preferred_element_type=jnp.float32,
    )
    rank = jnp.sum(jnp.where(hits, inside + base[:, :, None], 0.0), axis=0)
    return rank.reshape(count).astype(jnp.int32)


def split16(x, parts):
    pieces = []
    for _ in range(parts):
        piece = x.astype(jnp.bfloat16).astype(jnp.float32)
        pieces.append(piece)
        x = x - piece
    return pieces


def stack16(x, parts):
    pieces = split16(x, parts)
    rows = x.shape[0] * parts
    if rows % 16:
        pieces.append(jnp.zeros((16 - rows % 16, x.shape[1]), jnp.float32))
    return jnp.concatenate(pieces, axis=0).astype(jnp.bfloat16)


def cross_parts(a, b):
    return (
        a[1:2] * b[2:3] - a[2:3] * b[1:2],
        a[2:3] * b[0:1] - a[0:1] * b[2:3],
        a[0:1] * b[1:2] - a[1:2] * b[0:1],
    )


def box_body(center_ref, rows_ref, basis_ref, block_ref, wave_ref, lanes_ref, parts_ref):
    b = pl.program_id(0)
    count = rows_ref.shape[0]
    coef = basis_ref.shape[1]
    cx, cy, cz = center_ref[0, b], center_ref[1, b], center_ref[2, b]
    fx, fy, fz = basis_ref[0:1, :], basis_ref[1:2, :], basis_ref[2:3, :]
    phase = basis_ref[3:4, :]
    lanes = jnp.concatenate(
        [rows_ref[i * LANES : (i + 1) * LANES, :].T[:8] for i in range(count // LANES)], axis=1
    )
    lanes_ref[0] = lanes
    zero = jnp.zeros((1, count), jnp.float32)
    table = jnp.concatenate(
        [lanes[3:6], zero, *cross_parts(lanes[3:6], lanes[0:3]), zero], axis=0
    )
    parts = stack16(table, 3)
    parts_ref[0] = parts
    chunk = 32
    highs, lows = [], []
    for c in range(count // chunk):
        r = rows_ref[c * chunk : (c + 1) * chunk, :]
        turns = (
            fx * (r[:, 0:1] - cx) + fy * (r[:, 1:2] - cy) + fz * (r[:, 2:3] - cz) + phase
        )
        wave = cos_turns(turns)
        high = wave.astype(jnp.bfloat16)
        highs.append(high)
        lows.append((wave - high.astype(jnp.float32)).astype(jnp.bfloat16))
    high = jnp.concatenate(highs, axis=0)
    low = jnp.concatenate(lows, axis=0)
    wave_ref[:, :coef] = high
    wave_ref[:, coef:] = low
    sums = jnp.dot(parts, high, preferred_element_type=jnp.float32)
    sums = sums + jnp.dot(parts, low, preferred_element_type=jnp.float32)
    sums = sums[0:8] + sums[8:16] + sums[16:24]
    block_ref[0] = (
        basis_ref[4:5, :] * sums[0:1]
        + basis_ref[5:6, :] * sums[1:2]
        + basis_ref[6:7, :] * sums[2:3]
    )


def box_call(center, rows, basis, boxes, per_box):
    coef = basis.shape[1]
    return pl.pallas_call(
        box_body,
        grid=(boxes,),
        out_shape=(
            jax.ShapeDtypeStruct((boxes, 1, coef), jnp.float32),
            jax.ShapeDtypeStruct((boxes * per_box, 2 * coef), jnp.bfloat16),
            jax.ShapeDtypeStruct((boxes, 8, per_box), jnp.float32),
            jax.ShapeDtypeStruct((boxes, 32, per_box), jnp.bfloat16),
        ),
        in_specs=[
            pl.BlockSpec(memory_space=pltpu.SMEM),
            pl.BlockSpec((per_box, LANES), lambda b: (b, 0)),
            pl.BlockSpec((8, coef), lambda b: (0, 0)),
        ],
        out_specs=(
            pl.BlockSpec((1, 1, coef), lambda b: (b, 0, 0)),
            pl.BlockSpec((per_box, 2 * coef), lambda b: (b, 0)),
            pl.BlockSpec((1, 8, per_box), lambda b: (b, 0, 0)),
            pl.BlockSpec((1, 32, per_box), lambda b: (b, 0, 0)),
        ),
        compiler_params=pltpu.CompilerParams(vmem_limit_bytes=VMEM_LIMIT),
    )(center, rows, basis)


def velocity_body(near_ref, rows_ref, lanes_ref, parts_ref, wave_ref, exp_ref, dir_ref, out_ref):
    b = pl.program_id(0)
    per_box = wave_ref.shape[0]
    coef = dir_ref.shape[1]
    near_count = near_ref.shape[1]
    chunk = 32

    def pair_sums(j, target):
        tx, ty, tz = target[0:1], target[1:2], target[2:3]
        pieces = []
        for c in range(per_box // chunk):
            at = pl.multiple_of(j * per_box + c * chunk, chunk)
            s = rows_ref[pl.ds(at, chunk), :]
            dx = tx - s[:, 0:1]
            dy = ty - s[:, 1:2]
            dz = tz - s[:, 2:3]
            r = lax.rsqrt(dx * dx + dy * dy + dz * dz + core_square)
            pieces.append((r * r * r).astype(jnp.bfloat16))
        factor = jnp.concatenate(pieces, axis=0)
        return jnp.dot(parts_ref[j], factor, preferred_element_type=jnp.float32)

    def whole_box(count):
        target = lanes_ref[b]
        table = stack16(dir_ref[...] * exp_ref[0], 2)
        contract = (((1,), (1,)), ((), ()))
        far = lax.dot_general(
            table, wave_ref[:, :coef], contract, preferred_element_type=jnp.float32
        )
        far = far + lax.dot_general(
            table, wave_ref[:, coef:], contract, preferred_element_type=jnp.float32
        )
        far = far[0:8] + far[8:16]
        sums = pair_sums(near_ref[b, 0], target)
        for v in range(1, count):
            sums = sums + pair_sums(near_ref[b, v], target)
        sums = sums[0:8] + sums[8:16] + sums[16:24]
        near = jnp.concatenate(
            [*cross_parts(sums[0:3], target[0:3]), jnp.zeros((5, per_box), jnp.float32)], axis=0
        ) - jnp.concatenate([sums[4:7], jnp.zeros((5, per_box), jnp.float32)], axis=0)
        total = near * inv_four_pi + far
        for i in range(per_box // LANES):
            out_ref[i * LANES : (i + 1) * LANES, :] = lanes_to_rows(
                total[:, i * LANES : (i + 1) * LANES]
            )

    held = (near_ref[b, 0] >= 0).astype(jnp.int32)
    for v in range(1, near_count):
        held = held + (near_ref[b, v] >= 0).astype(jnp.int32)
    for count in range(1, near_count + 1):
        pl.when(held == count)(functools.partial(whole_box, count))


def velocity_call(near, rows, lanes, parts, wave, exps, basis_dir, boxes, per_box):
    coef = basis_dir.shape[1]
    return pl.pallas_call(
        velocity_body,
        grid=(boxes,),
        out_shape=jax.ShapeDtypeStruct((boxes * per_box, LANES), jnp.float32),
        in_specs=[
            pl.BlockSpec(memory_space=pltpu.SMEM),
            pl.BlockSpec(memory_space=pltpu.VMEM),
            pl.BlockSpec(memory_space=pltpu.VMEM),
            pl.BlockSpec(memory_space=pltpu.VMEM),
            pl.BlockSpec((per_box, 2 * coef), lambda b: (b, 0)),
            pl.BlockSpec((1, 1, coef), lambda b: (b, 0, 0)),
            pl.BlockSpec(memory_space=pltpu.VMEM),
        ],
        out_specs=pl.BlockSpec((per_box, LANES), lambda b: (b, 0)),
        compiler_params=pltpu.CompilerParams(vmem_limit_bytes=VMEM_LIMIT),
    )(near, rows, lanes, parts, wave, exps, basis_dir)


def per_device(
    n_age,
    n_box,
    position,
    strength,
    node_box,
    box_order,
    box_center,
    near_list,
    m2l_source,
    m2l_type,
    basis_dir,
    basis_freq,
    basis_phase,
    translation,
):
    groups = n_age * n_box
    node_count = position.shape[1]
    box_local = box_order.shape[0]
    slots_total = 2 * node_count
    per_peer = slots_total // groups
    per_box = slots_total // box_local
    coef = basis_phase.shape[0]
    kind_count = translation.shape[0]
    box_total = groups * box_local

    padded_order = jnp.pad(box_order, (0, LANES - box_local)).reshape(1, LANES)
    all_order = gather_blocks(padded_order, n_age, n_box, 0)[:, :, 0, :box_local].reshape(-1)

    node_slot = jnp.sum(
        jnp.where(
            node_box[None, :] == all_order[:, None],
            jnp.arange(box_total, dtype=jnp.int32)[:, None],
            0,
        ),
        axis=0,
    )
    owner = node_slot // box_local
    label = (node_slot - owner * box_local + 1).astype(jnp.float32)
    send_at = owner * per_peer + ranks(owner, groups)
    fields = jnp.concatenate(
        [position, strength, label[None, :], jnp.zeros((1, node_count), jnp.float32)], axis=0
    )
    payload = permute_call(
        spread_body, send_at, fields, (8, slots_total), (node_count, slots_total)
    )
    got = lax.all_to_all(payload, AXES, split_axis=1, concat_axis=1, tiled=True)

    hit_source = (m2l_source[:, :, None] == all_order[None, None, :]).astype(jnp.bfloat16)
    kind_hits = (
        m2l_type[:, :, None] == jnp.arange(kind_count, dtype=jnp.int32)[None, None, :]
    ).astype(jnp.bfloat16)
    list_counts = jnp.einsum(
        "jlt,jlb->tjb", kind_hits, hit_source, preferred_element_type=jnp.float32
    )
    list_counts = list_counts.astype(jnp.bfloat16).reshape(kind_count * box_local, box_total)
    near_local = jnp.sum(
        jnp.where(
            near_list[:, :, None] == box_order[None, None, :],
            jnp.arange(1, box_local + 1, dtype=jnp.int32)[None, None, :],
            0,
        ),
        axis=2,
    ) - 1

    got_label = got[6].astype(jnp.int32) - 1
    live = got_label >= 0
    tile_at = jnp.where(
        live, got_label * per_box + ranks(got_label, box_local), slots_total
    )
    rows = permute_call(group_body, tile_at, got, (slots_total + 8, LANES), (slots_total,))
    basis = jnp.concatenate(
        [
            basis_freq * inv_two_pi,
            basis_phase[None, :] * inv_two_pi,
            basis_dir,
            jnp.zeros((1, coef), jnp.float32),
        ],
        axis=0,
    )
    sums, wave, lanes, parts = box_call(box_center, rows, basis, box_local, per_box)
    local_blocks = sums.reshape(box_local, coef).astype(jnp.bfloat16)
    all_blocks = gather_blocks(local_blocks, n_age, n_box, 1).reshape(box_total, coef)
    mixed = jnp.dot(list_counts, all_blocks, preferred_element_type=jnp.float32)
    mixed = mixed.astype(jnp.bfloat16).reshape(kind_count, box_local, coef)
    expansions = jnp.einsum(
        "tjc,tkc->jk", mixed, translation, preferred_element_type=jnp.float32
    )
    dir_rows = jnp.pad(basis_dir, ((0, 5), (0, 0)))
    vel_rows = velocity_call(
        near_local,
        rows,
        lanes,
        parts,
        wave,
        expansions.reshape(box_local, 1, coef),
        dir_rows,
        box_local,
        per_box,
    )
    back = permute_call(
        ungroup_body,
        jnp.minimum(tile_at, slots_total - 1),
        vel_rows,
        (8, slots_total),
        (slots_total,),
    )
    returned = lax.all_to_all(back[:3], AXES, split_axis=1, concat_axis=1, tiled=True)
    returned = jnp.pad(returned, ((0, 5), (0, 0)))
    out = permute_call(
        collect_body, send_at, returned, (8, node_count), (slots_total, node_count)
    )
    return out[:3]


def solution(mesh):
    n_box = mesh.shape["box"]
    n_age = mesh.shape["age"]
    placed = (
        P(None, AXES),
        P(None, AXES),
        P(AXES),
        P(AXES),
        P(None, AXES),
        P(AXES, None),
        P(AXES, None),
        P(AXES, None),
        P(),
        P(),
        P(),
        P(),
    )
    return jax.shard_map(
        functools.partial(per_device, n_age, n_box),
        mesh=mesh,
        in_specs=placed,
        out_specs=P(None, AXES),
        check_vma=False,
    )
```

```python
import functools

import jax
import jax.numpy as jnp
import numpy as np
from jax import lax
from jax.experimental import pallas as pl
from jax.experimental.pallas import tpu as pltpu
from jax.sharding import PartitionSpec as P

AXES = ("age", "box")
core_square = 0.01
inv_four_pi = 0.07957747154594767
inv_two_pi = 0.15915494309189535
LANES = 128
VMEM_LIMIT = 32 * 1024 * 1024


def cos_coefficients(degree):
    nodes = np.cos(np.pi * (np.arange(64) + 0.5) / 64)
    w = 0.125 * (nodes + 1.0)
    fit = np.polynomial.chebyshev.Chebyshev.fit(
        w, np.cos(2 * np.pi * np.sqrt(w)), degree, domain=[0, 0.25]
    )
    return [float(c) for c in fit.convert(kind=np.polynomial.Polynomial).coef]


COS_COEF = cos_coefficients(6)


def cos_turns(turns):
    v = turns - ((turns + 12582912.0) - 12582912.0)
    w = v * v
    acc = jnp.full_like(w, COS_COEF[-1])
    for c in COS_COEF[-2::-1]:
        acc = acc * w + c
    return acc


def gather_body(n_age, n_box, x_ref, o_ref, send_sem, recv_sem):
    me_age, me_box = lax.axis_index("age"), lax.axis_index("box")
    barrier = pltpu.get_barrier_semaphore()

    def on_box(d):
        return {"age": me_age, "box": lax.rem(me_box + d, n_box)}

    def on_age(d):
        return {"age": lax.rem(me_age + d, n_age), "box": me_box}

    def greet(peer):
        def step(d, carry):
            pl.semaphore_signal(
                barrier, inc=1, device_id=peer(d), device_id_type=pl.DeviceIdType.MESH
            )
            return carry

        return step

    lax.fori_loop(1, n_box, greet(on_box), 0)
    lax.fori_loop(1, n_age, greet(on_age), 0)
    o_ref[me_age, me_box] = x_ref[...]
    pl.semaphore_wait(barrier, n_box - 1 + n_age - 1)

    def along_box(d):
        return pltpu.make_async_remote_copy(
            src_ref=x_ref,
            dst_ref=o_ref.at[me_age, me_box],
            send_sem=send_sem.at[d - 1],
            recv_sem=recv_sem.at[d - 1],
            device_id=on_box(d),
            device_id_type=pl.DeviceIdType.MESH,
        )

    def along_age(d):
        return pltpu.make_async_remote_copy(
            src_ref=o_ref.at[me_age],
            dst_ref=o_ref.at[me_age],
            send_sem=send_sem.at[n_box - 2 + d],
            recv_sem=recv_sem.at[n_box - 2 + d],
            device_id=on_age(d),
            device_id_type=pl.DeviceIdType.MESH,
        )

    def start(copy):
        def step(d, carry):
            copy(d).start()
            return carry

        return step

    def finish(copy):
        def step(d, carry):
            copy(d).wait()
            return carry

        return step

    lax.fori_loop(1, n_box, start(along_box), 0)
    lax.fori_loop(1, n_box, finish(along_box), 0)
    lax.fori_loop(1, n_age, start(along_age), 0)
    lax.fori_loop(1, n_age, finish(along_age), 0)


def gather_blocks(x, n_age, n_box, collective_id):
    copies = n_age + n_box - 2
    return pl.pallas_call(
        functools.partial(gather_body, n_age, n_box),
        out_shape=jax.ShapeDtypeStruct((n_age, n_box) + x.shape, x.dtype),
        in_specs=[pl.BlockSpec(memory_space=pltpu.VMEM)],
        out_specs=pl.BlockSpec(memory_space=pltpu.VMEM),
        scratch_shapes=[
            pltpu.SemaphoreType.DMA((copies,)),
            pltpu.SemaphoreType.DMA((copies,)),
        ],
        compiler_params=pltpu.CompilerParams(
            collective_id=collective_id, has_side_effects=True
        ),
    )(x)


def lanes_to_rows(tile):
    padded = jnp.concatenate([tile, jnp.zeros((LANES - tile.shape[0], LANES), tile.dtype)], axis=0)
    return padded.T


def fill_rows(src_ref, rows_ref, count):
    def step(i, carry):
        at = pl.multiple_of(i * LANES, LANES)
        rows_ref[pl.ds(at, LANES), :] = lanes_to_rows(src_ref[:, pl.ds(at, LANES)])
        return carry

    lax.fori_loop(0, count // LANES, step, 0, unroll=8)


def take_lanes(rows_ref, out_ref, count):
    def step(i, carry):
        at = pl.multiple_of(i * LANES, LANES)
        out_ref[:, pl.ds(at, LANES)] = rows_ref[pl.ds(at, LANES), :].T[: out_ref.shape[0]]
        return carry

    lax.fori_loop(0, count // LANES, step, 0, unroll=8)


def zero_rows(ref):
    def step(i, carry):
        at = pl.multiple_of(i * 8, 8)
        ref[pl.ds(at, 8), :] = jnp.zeros((8, LANES), jnp.float32)
        return carry

    lax.fori_loop(0, ref.shape[0] // 8, step, 0, unroll=8)


def scatter_rows(idx_ref, src_ref, dst_ref, count):
    def step(i, carry):
        at = pl.multiple_of(i * 16, 16)
        block = src_ref[pl.ds(at, 16), :]
        for u in range(16):
            dst_ref[pl.ds(idx_ref[at + u], 1), :] = block[u : u + 1, :]
        return carry

    lax.fori_loop(0, count // 16, step, 0)


def gather_rows(idx_ref, src_ref, dst_ref, count):
    def step(i, carry):
        at = pl.multiple_of(i * 16, 16)
        rows = [src_ref[pl.ds(idx_ref[at + u], 1), :] for u in range(16)]
        dst_ref[pl.ds(at, 16), :] = jnp.concatenate(rows, axis=0)
        return carry

    lax.fori_loop(0, count // 16, step, 0)


def spread_body(idx_ref, x_ref, out_ref, rows, placed):
    fill_rows(x_ref, rows, x_ref.shape[1])
    zero_rows(placed)
    scatter_rows(idx_ref, rows, placed, x_ref.shape[1])
    take_lanes(placed, out_ref, out_ref.shape[1])


def collect_body(idx_ref, x_ref, out_ref, src, rows):
    fill_rows(x_ref, src, x_ref.shape[1])
    gather_rows(idx_ref, src, rows, out_ref.shape[1])
    take_lanes(rows, out_ref, out_ref.shape[1])


def permute_call(body, idx, x, out_shape, scratch_rows):
    return pl.pallas_call(
        body,
        out_shape=jax.ShapeDtypeStruct(out_shape, jnp.float32),
        in_specs=[
            pl.BlockSpec(memory_space=pltpu.SMEM),
            pl.BlockSpec(memory_space=pltpu.VMEM),
        ],
        out_specs=pl.BlockSpec(memory_space=pltpu.VMEM),
        scratch_shapes=[pltpu.VMEM((r, LANES), jnp.float32) for r in scratch_rows],
        compiler_params=pltpu.CompilerParams(vmem_limit_bytes=VMEM_LIMIT),
    )(idx, x)


def ranks(key, kinds):
    count = key.shape[0]
    blocks = count // LANES
    hits = (key[None, :] == jnp.arange(kinds, dtype=jnp.int32)[:, None]).reshape(
        kinds, blocks, LANES
    )
    hits16 = hits.astype(jnp.bfloat16)
    lane = np.arange(LANES)
    before = jnp.asarray(lane[:, None] < lane[None, :], jnp.bfloat16)
    inside = jnp.dot(
        hits16.reshape(kinds * blocks, LANES), before, preferred_element_type=jnp.float32
    ).reshape(kinds, blocks, LANES)
    totals = jnp.sum(hits.astype(jnp.float32), axis=2)
    block = np.arange(blocks)
    base = jnp.dot(
        totals.astype(jnp.bfloat16),
        jnp.asarray(block[:, None] < block[None, :], jnp.bfloat16),
        preferred_element_type=jnp.float32,
    )
    rank = jnp.sum(jnp.where(hits, inside + base[:, :, None], 0.0), axis=0)
    return rank.reshape(count).astype(jnp.int32)


def split16(x, parts):
    pieces = []
    for _ in range(parts):
        piece = x.astype(jnp.bfloat16).astype(jnp.float32)
        pieces.append(piece)
        x = x - piece
    return pieces


def stack16(x, parts):
    pieces = split16(x, parts)
    rows = x.shape[0] * parts
    if rows % 16:
        pieces.append(jnp.zeros((16 - rows % 16, x.shape[1]), jnp.float32))
    return jnp.concatenate(pieces, axis=0).astype(jnp.bfloat16)


def cross_parts(a, b):
    return (
        a[1:2] * b[2:3] - a[2:3] * b[1:2],
        a[2:3] * b[0:1] - a[0:1] * b[2:3],
        a[0:1] * b[1:2] - a[1:2] * b[0:1],
    )


def one_box(b, center_ref, basis_ref, freq_ref, rows_ref, block_ref, wave_ref, lanes_ref, parts_ref):
    count = lanes_ref.shape[2]
    at = pl.multiple_of(b * count, count)
    coef = basis_ref.shape[1]
    cx, cy, cz = center_ref[0, b], center_ref[1, b], center_ref[2, b]
    lanes = jnp.concatenate(
        [rows_ref[pl.ds(at + i * LANES, LANES), :].T[:8] for i in range(count // LANES)], axis=1
    )
    lanes_ref[b] = lanes
    zero = jnp.zeros((1, count), jnp.float32)
    table = jnp.concatenate(
        [lanes[3:6], zero, *cross_parts(lanes[3:6], lanes[0:3]), zero], axis=0
    )
    parts = stack16(table, 3)
    parts_ref[b] = parts
    one = jnp.ones((1, count), jnp.float32)
    offset = jnp.concatenate(
        [lanes[0:1] - cx, lanes[1:2] - cy, lanes[2:3] - cz, one, jnp.zeros((4, count), jnp.float32)],
        axis=0,
    )
    o1, o2, o3 = split16(offset, 3)
    stacked = jnp.concatenate([o3, o2, o2, o1, o1, o1], axis=0).astype(jnp.bfloat16)
    turns = lax.dot_general(
        stacked, freq_ref[...], (((0,), (0,)), ((), ())), preferred_element_type=jnp.float32
    )
    chunk = 32
    highs, lows = [], []
    for c in range(count // chunk):
        wave = cos_turns(turns[c * chunk : (c + 1) * chunk])
        high = wave.astype(jnp.bfloat16)
        highs.append(high)
        lows.append((wave - high.astype(jnp.float32)).astype(jnp.bfloat16))
    high = jnp.concatenate(highs, axis=0)
    low = jnp.concatenate(lows, axis=0)
    wave_ref[pl.ds(at, count), :coef] = high
    wave_ref[pl.ds(at, count), coef:] = low
    sums = jnp.dot(parts, high, preferred_element_type=jnp.float32)
    sums = sums + jnp.dot(parts, low, preferred_element_type=jnp.float32)
    sums = sums[0:8] + sums[8:16] + sums[16:24]
    block_ref[b] = (
        basis_ref[0:1, :] * sums[0:1]
        + basis_ref[1:2, :] * sums[1:2]
        + basis_ref[2:3, :] * sums[2:3]
    )


def group_body(
    idx_ref, center_ref, x_ref, basis_ref, freq_ref,
    rows_ref, block_ref, wave_ref, lanes_ref, parts_ref, scattered,
):
    fill_rows(x_ref, scattered, x_ref.shape[1])
    zero_rows(rows_ref)
    scatter_rows(idx_ref, scattered, rows_ref, x_ref.shape[1])

    def step(b, carry):
        one_box(
            b, center_ref, basis_ref, freq_ref, rows_ref, block_ref, wave_ref, lanes_ref, parts_ref
        )
        return carry

    lax.fori_loop(0, block_ref.shape[0], step, 0, unroll=2)


def split_body(x_ref, out_ref):
    f1, f2, f3 = split16(x_ref[...], 3)
    out_ref[...] = jnp.concatenate([f1, f2, f1, f3, f2, f1], axis=0).astype(jnp.bfloat16)


def split_call(x):
    return pl.pallas_call(
        split_body, out_shape=jax.ShapeDtypeStruct((6 * x.shape[0], x.shape[1]), jnp.bfloat16)
    )(x)


def group_call(idx, center, got, basis, freq, boxes, per_box):
    coef = basis.shape[1]
    slots = boxes * per_box
    return pl.pallas_call(
        group_body,
        out_shape=(
            jax.ShapeDtypeStruct((slots + 8, LANES), jnp.float32),
            jax.ShapeDtypeStruct((boxes, 1, coef), jnp.float32),
            jax.ShapeDtypeStruct((slots, 2 * coef), jnp.bfloat16),
            jax.ShapeDtypeStruct((boxes, 8, per_box), jnp.float32),
            jax.ShapeDtypeStruct((boxes, 32, per_box), jnp.bfloat16),
        ),
        in_specs=[pl.BlockSpec(memory_space=pltpu.SMEM)] * 2
        + [pl.BlockSpec(memory_space=pltpu.VMEM)] * 3,
        out_specs=(pl.BlockSpec(memory_space=pltpu.VMEM),) * 5,
        scratch_shapes=[pltpu.VMEM((slots, LANES), jnp.float32)],
        compiler_params=pltpu.CompilerParams(vmem_limit_bytes=VMEM_LIMIT),
    )(idx, center, got, basis, freq)


def one_velocity(b, near_ref, rows_ref, lanes_ref, parts_ref, wave_ref, exp_ref, dir_ref, out_ref):
    per_box = lanes_ref.shape[2]
    here = pl.multiple_of(b * per_box, per_box)
    coef = dir_ref.shape[1]
    near_count = near_ref.shape[1]
    chunk = 32

    def pair_sums(j, target):
        tx, ty, tz = target[0:1], target[1:2], target[2:3]
        pieces = []
        for c in range(per_box // chunk):
            at = pl.multiple_of(j * per_box + c * chunk, chunk)
            s = rows_ref[pl.ds(at, chunk), :]
            dx = tx - s[:, 0:1]
            dy = ty - s[:, 1:2]
            dz = tz - s[:, 2:3]
            r = lax.rsqrt(dx * dx + dy * dy + dz * dz + core_square)
            pieces.append((r * r * r).astype(jnp.bfloat16))
        factor = jnp.concatenate(pieces, axis=0)
        return jnp.dot(parts_ref[j], factor, preferred_element_type=jnp.float32)

    def whole_box(count):
        target = lanes_ref[b]
        table = stack16(dir_ref[...] * exp_ref[b], 2)
        contract = (((1,), (1,)), ((), ()))
        far = lax.dot_general(
            table, wave_ref[pl.ds(here, per_box), :coef], contract, preferred_element_type=jnp.float32
        )
        far = far + lax.dot_general(
            table, wave_ref[pl.ds(here, per_box), coef:], contract, preferred_element_type=jnp.float32
        )
        far = far[0:8] + far[8:16]
        sums = pair_sums(near_ref[b, 0], target)
        for v in range(1, count):
            sums = sums + pair_sums(near_ref[b, v], target)
        sums = sums[0:8] + sums[8:16] + sums[16:24]
        near = jnp.concatenate(
            [*cross_parts(sums[0:3], target[0:3]), jnp.zeros((5, per_box), jnp.float32)], axis=0
        ) - jnp.concatenate([sums[4:7], jnp.zeros((5, per_box), jnp.float32)], axis=0)
        total = near * inv_four_pi + far
        for i in range(per_box // LANES):
            out_ref[pl.ds(here + i * LANES, LANES), :] = lanes_to_rows(
                total[:, i * LANES : (i + 1) * LANES]
            )

    held = (near_ref[b, 0] >= 0).astype(jnp.int32)
    for v in range(1, near_count):
        held = held + (near_ref[b, v] >= 0).astype(jnp.int32)
    for count in range(1, near_count + 1):
        pl.when(held == count)(functools.partial(whole_box, count))


def velocity_body(
    idx_ref, near_ref, rows_ref, lanes_ref, parts_ref, wave_ref, exp_ref, dir_ref,
    out_ref, vel, rows,
):
    def step(b, carry):
        one_velocity(
            b, near_ref, rows_ref, lanes_ref, parts_ref, wave_ref, exp_ref, dir_ref, vel
        )
        return carry

    lax.fori_loop(0, lanes_ref.shape[0], step, 0)
    gather_rows(idx_ref, vel, rows, out_ref.shape[1])
    take_lanes(rows, out_ref, out_ref.shape[1])


def velocity_call(idx, near, rows, lanes, parts, wave, exps, basis_dir):
    slots = wave.shape[0]
    return pl.pallas_call(
        velocity_body,
        out_shape=jax.ShapeDtypeStruct((8, slots), jnp.float32),
        in_specs=[pl.BlockSpec(memory_space=pltpu.SMEM)] * 2
        + [pl.BlockSpec(memory_space=pltpu.VMEM)] * 6,
        out_specs=pl.BlockSpec(memory_space=pltpu.VMEM),
        scratch_shapes=[pltpu.VMEM((slots, LANES), jnp.float32)] * 2,
        compiler_params=pltpu.CompilerParams(vmem_limit_bytes=VMEM_LIMIT),
    )(idx, near, rows, lanes, parts, wave, exps, basis_dir)


def per_device(
    n_age,
    n_box,
    position,
    strength,
    node_box,
    box_order,
    box_center,
    near_list,
    m2l_source,
    m2l_type,
    basis_dir,
    basis_freq,
    basis_phase,
    translation,
):
    groups = n_age * n_box
    node_count = position.shape[1]
    box_local = box_order.shape[0]
    slots_total = 2 * node_count
    per_peer = slots_total // groups
    per_box = slots_total // box_local
    coef = basis_phase.shape[0]
    kind_count = translation.shape[0]
    box_total = groups * box_local

    padded_order = jnp.pad(box_order, (0, LANES - box_local)).reshape(1, LANES)
    all_order = gather_blocks(padded_order, n_age, n_box, 0)[:, :, 0, :box_local].reshape(-1)

    node_slot = jnp.sum(
        jnp.where(
            node_box[None, :] == all_order[:, None],
            jnp.arange(box_total, dtype=jnp.int32)[:, None],
            0,
        ),
        axis=0,
    )
    owner = node_slot // box_local
    label = (node_slot - owner * box_local + 1).astype(jnp.float32)
    send_at = owner * per_peer + ranks(owner, groups)
    fields = jnp.concatenate(
        [position, strength, label[None, :], jnp.zeros((1, node_count), jnp.float32)], axis=0
    )
    payload = permute_call(
        spread_body, send_at, fields, (8, slots_total), (node_count, slots_total)
    )
    got = lax.all_to_all(payload, AXES, split_axis=1, concat_axis=1, tiled=True)

    hit_source = (m2l_source[:, :, None] == all_order[None, None, :]).astype(jnp.bfloat16)
    kind_hits = (
        m2l_type[:, :, None] == jnp.arange(kind_count, dtype=jnp.int32)[None, None, :]
    ).astype(jnp.bfloat16)
    list_counts = jnp.einsum(
        "jlt,jlb->tjb", kind_hits, hit_source, preferred_element_type=jnp.float32
    )
    list_counts = list_counts.astype(jnp.bfloat16).reshape(kind_count * box_local, box_total)
    near_local = jnp.sum(
        jnp.where(
            near_list[:, :, None] == box_order[None, None, :],
            jnp.arange(1, box_local + 1, dtype=jnp.int32)[None, None, :],
            0,
        ),
        axis=2,
    ) - 1

    got_label = got[6].astype(jnp.int32) - 1
    live = got_label >= 0
    tile_at = jnp.where(
        live, got_label * per_box + ranks(got_label, box_local), slots_total
    )
    dir_rows = jnp.pad(basis_dir, ((0, 5), (0, 0)))
    waves = jnp.concatenate([basis_freq, basis_phase[None, :]], axis=0) * inv_two_pi
    freq = split_call(jnp.pad(waves, ((0, 4), (0, 0))))
    rows, sums, wave, lanes, parts = group_call(
        tile_at, box_center, got, dir_rows, freq, box_local, per_box
    )
    local_blocks = sums.reshape(box_local, coef).astype(jnp.bfloat16)
    all_blocks = gather_blocks(local_blocks, n_age, n_box, 1).reshape(box_total, coef)
    mixed = jnp.dot(list_counts, all_blocks, preferred_element_type=jnp.float32)
    mixed = mixed.astype(jnp.bfloat16).reshape(kind_count, box_local, coef)
    expansions = jnp.einsum(
        "tjc,tkc->jk", mixed, translation, preferred_element_type=jnp.float32
    )
    back = velocity_call(
        jnp.minimum(tile_at, slots_total - 1),
        near_local,
        rows,
        lanes,
        parts,
        wave,
        expansions.reshape(box_local, 1, coef),
        dir_rows,
    )
    returned = lax.all_to_all(back[:3], AXES, split_axis=1, concat_axis=1, tiled=True)
    returned = jnp.pad(returned, ((0, 5), (0, 0)))
    out = permute_call(
        collect_body, send_at, returned, (8, node_count), (slots_total, node_count)
    )
    return out[:3]


def solution(mesh):
    n_box = mesh.shape["box"]
    n_age = mesh.shape["age"]
    placed = (
        P(None, AXES),
        P(None, AXES),
        P(AXES),
        P(AXES),
        P(None, AXES),
        P(AXES, None),
        P(AXES, None),
        P(AXES, None),
        P(),
        P(),
        P(),
        P(),
    )
    return jax.shard_map(
        functools.partial(per_device, n_age, n_box),
        mesh=mesh,
        in_specs=placed,
        out_specs=P(None, AXES),
        check_vma=False,
    )
```

```python
import functools

import jax
import jax.numpy as jnp
import numpy as np
from jax import lax
from jax.experimental import pallas as pl
from jax.experimental.pallas import tpu as pltpu
from jax.sharding import PartitionSpec as P

AXES = ("age", "box")
core_square = 0.01
inv_four_pi = 0.07957747154594767
inv_two_pi = 0.15915494309189535
LANES = 128
VMEM_LIMIT = 32 * 1024 * 1024
SMALL_LIMIT = 6 * 1024 * 1024


def cos_coefficients(degree):
    nodes = np.cos(np.pi * (np.arange(64) + 0.5) / 64)
    w = 0.125 * (nodes + 1.0)
    fit = np.polynomial.chebyshev.Chebyshev.fit(
        w, np.cos(2 * np.pi * np.sqrt(w)), degree, domain=[0, 0.25]
    )
    return [float(c) for c in fit.convert(kind=np.polynomial.Polynomial).coef]


COS_COEF = cos_coefficients(6)


def cos_turns(turns):
    v = turns - ((turns + 12582912.0) - 12582912.0)
    w = v * v
    acc = jnp.full_like(w, COS_COEF[-1])
    for c in COS_COEF[-2::-1]:
        acc = acc * w + c
    return acc


def gather_body(n_age, n_box, x_ref, o_ref, send_sem, recv_sem):
    me_age, me_box = lax.axis_index("age"), lax.axis_index("box")
    barrier = pltpu.get_barrier_semaphore()

    def on_box(d):
        return {"age": me_age, "box": lax.rem(me_box + d, n_box)}

    def on_age(d):
        return {"age": lax.rem(me_age + d, n_age), "box": me_box}

    def greet(peer):
        def step(d, carry):
            pl.semaphore_signal(
                barrier, inc=1, device_id=peer(d), device_id_type=pl.DeviceIdType.MESH
            )
            return carry

        return step

    lax.fori_loop(1, n_box, greet(on_box), 0)
    lax.fori_loop(1, n_age, greet(on_age), 0)
    o_ref[me_age, me_box] = x_ref[...]
    pl.semaphore_wait(barrier, n_box - 1 + n_age - 1)

    def along_box(d):
        return pltpu.make_async_remote_copy(
            src_ref=x_ref,
            dst_ref=o_ref.at[me_age, me_box],
            send_sem=send_sem.at[d - 1],
            recv_sem=recv_sem.at[d - 1],
            device_id=on_box(d),
            device_id_type=pl.DeviceIdType.MESH,
        )

    def along_age(d):
        return pltpu.make_async_remote_copy(
            src_ref=o_ref.at[me_age],
            dst_ref=o_ref.at[me_age],
            send_sem=send_sem.at[n_box - 2 + d],
            recv_sem=recv_sem.at[n_box - 2 + d],
            device_id=on_age(d),
            device_id_type=pl.DeviceIdType.MESH,
        )

    def start(copy):
        def step(d, carry):
            copy(d).start()
            return carry

        return step

    def finish(copy):
        def step(d, carry):
            copy(d).wait()
            return carry

        return step

    lax.fori_loop(1, n_box, start(along_box), 0)
    lax.fori_loop(1, n_box, finish(along_box), 0)
    lax.fori_loop(1, n_age, start(along_age), 0)
    lax.fori_loop(1, n_age, finish(along_age), 0)


def gather_blocks(x, n_age, n_box, collective_id):
    copies = n_age + n_box - 2
    return pl.pallas_call(
        functools.partial(gather_body, n_age, n_box),
        out_shape=jax.ShapeDtypeStruct((n_age, n_box) + x.shape, x.dtype),
        in_specs=[pl.BlockSpec(memory_space=pltpu.VMEM)],
        out_specs=pl.BlockSpec(memory_space=pltpu.VMEM),
        scratch_shapes=[
            pltpu.SemaphoreType.DMA((copies,)),
            pltpu.SemaphoreType.DMA((copies,)),
        ],
        compiler_params=pltpu.CompilerParams(
            collective_id=collective_id, has_side_effects=True, vmem_limit_bytes=SMALL_LIMIT
        ),
    )(x)


def exchange_body(n_box, n, x_ref, o_ref, send_sem, recv_sem):
    me = lax.axis_index("age") * n_box + lax.axis_index("box")
    barrier = pltpu.get_barrier_semaphore()

    def place(other):
        return {"age": other // n_box, "box": lax.rem(other, n_box)}

    def greet(d, carry):
        pl.semaphore_signal(
            barrier,
            inc=1,
            device_id=place(lax.rem(me + d, n)),
            device_id_type=pl.DeviceIdType.MESH,
        )
        return carry

    lax.fori_loop(1, n, greet, 0)
    o_ref[me] = x_ref[me]
    pl.semaphore_wait(barrier, n - 1)

    def copy(d):
        other = lax.rem(me + d, n)
        return pltpu.make_async_remote_copy(
            src_ref=x_ref.at[other],
            dst_ref=o_ref.at[me],
            send_sem=send_sem.at[d - 1],
            recv_sem=recv_sem.at[d - 1],
            device_id=place(other),
            device_id_type=pl.DeviceIdType.MESH,
        )

    def send(d, carry):
        copy(d).start()
        return carry

    def finish(d, carry):
        copy(d).wait()
        return carry

    lax.fori_loop(1, n, send, 0)
    lax.fori_loop(1, n, finish, 0)


def exchange(x, n_box, collective_id):
    n = x.shape[0]
    return pl.pallas_call(
        functools.partial(exchange_body, n_box, n),
        out_shape=jax.ShapeDtypeStruct(x.shape, x.dtype),
        in_specs=[pl.BlockSpec(memory_space=pltpu.VMEM)],
        out_specs=pl.BlockSpec(memory_space=pltpu.VMEM),
        scratch_shapes=[
            pltpu.SemaphoreType.DMA((n - 1,)),
            pltpu.SemaphoreType.DMA((n - 1,)),
        ],
        compiler_params=pltpu.CompilerParams(
            collective_id=collective_id, has_side_effects=True, vmem_limit_bytes=SMALL_LIMIT
        ),
    )(x)


def load_lanes(ref, i):
    if len(ref.shape) == 2:
        return ref[:, pl.ds(pl.multiple_of(i * LANES, LANES), LANES)]
    per = ref.shape[2]
    if per >= LANES:
        k = per // LANES
        return ref[i // k, :, pl.ds(pl.multiple_of(lax.rem(i, k) * LANES, LANES), LANES)]
    m = LANES // per
    return jnp.concatenate([ref[i * m + u] for u in range(m)], axis=1)


def store_lanes(ref, i, tile):
    if len(ref.shape) == 2:
        ref[:, pl.ds(pl.multiple_of(i * LANES, LANES), LANES)] = tile
        return
    per = ref.shape[2]
    if per >= LANES:
        k = per // LANES
        ref[i // k, :, pl.ds(pl.multiple_of(lax.rem(i, k) * LANES, LANES), LANES)] = tile
        return
    m = LANES // per
    for u in range(m):
        ref[i * m + u] = tile[:, u * per : (u + 1) * per]


def columns(ref):
    return ref.shape[-1] if len(ref.shape) == 2 else ref.shape[0] * ref.shape[2]


def lanes_to_rows(tile):
    padded = jnp.concatenate([tile, jnp.zeros((LANES - tile.shape[0], LANES), tile.dtype)], axis=0)
    return padded.T


def fill_rows(src_ref, rows_ref, count):
    def step(i, carry):
        at = pl.multiple_of(i * LANES, LANES)
        rows_ref[pl.ds(at, LANES), :] = lanes_to_rows(load_lanes(src_ref, i))
        return carry

    lax.fori_loop(0, count // LANES, step, 0, unroll=8)


def take_lanes(rows_ref, out_ref, count):
    def step(i, carry):
        at = pl.multiple_of(i * LANES, LANES)
        store_lanes(out_ref, i, rows_ref[pl.ds(at, LANES), :].T[:8])
        return carry

    lax.fori_loop(0, count // LANES, step, 0, unroll=8)


def zero_rows(ref):
    def step(i, carry):
        at = pl.multiple_of(i * 8, 8)
        ref[pl.ds(at, 8), :] = jnp.zeros((8, LANES), jnp.float32)
        return carry

    lax.fori_loop(0, ref.shape[0] // 8, step, 0, unroll=8)


def scatter_rows(idx_ref, src_ref, dst_ref, count):
    def step(i, carry):
        at = pl.multiple_of(i * 16, 16)
        block = src_ref[pl.ds(at, 16), :]
        for u in range(16):
            dst_ref[pl.ds(idx_ref[at + u], 1), :] = block[u : u + 1, :]
        return carry

    lax.fori_loop(0, count // 16, step, 0)


def gather_rows(idx_ref, src_ref, dst_ref, count):
    def step(i, carry):
        at = pl.multiple_of(i * 16, 16)
        rows = [src_ref[pl.ds(idx_ref[at + u], 1), :] for u in range(16)]
        dst_ref[pl.ds(at, 16), :] = jnp.concatenate(rows, axis=0)
        return carry

    lax.fori_loop(0, count // 16, step, 0)


def spread_body(idx_ref, x_ref, out_ref, rows, placed):
    fill_rows(x_ref, rows, columns(x_ref))
    zero_rows(placed)
    scatter_rows(idx_ref, rows, placed, columns(x_ref))
    take_lanes(placed, out_ref, columns(out_ref))


def collect_body(idx_ref, x_ref, out_ref, src, rows):
    fill_rows(x_ref, src, columns(x_ref))
    gather_rows(idx_ref, src, rows, columns(out_ref))
    take_lanes(rows, out_ref, columns(out_ref))


def permute_call(body, idx, x, out_shape, scratch_rows):
    return pl.pallas_call(
        body,
        out_shape=jax.ShapeDtypeStruct(out_shape, jnp.float32),
        in_specs=[
            pl.BlockSpec(memory_space=pltpu.SMEM),
            pl.BlockSpec(memory_space=pltpu.VMEM),
        ],
        out_specs=pl.BlockSpec(memory_space=pltpu.VMEM),
        scratch_shapes=[pltpu.VMEM((r, LANES), jnp.float32) for r in scratch_rows],
        compiler_params=pltpu.CompilerParams(vmem_limit_bytes=VMEM_LIMIT),
    )(idx, x)


def ranks(key, kinds):
    count = key.shape[0]
    blocks = count // LANES
    hits = (key[None, :] == jnp.arange(kinds, dtype=jnp.int32)[:, None]).reshape(
        kinds, blocks, LANES
    )
    hits16 = hits.astype(jnp.bfloat16)
    lane = np.arange(LANES)
    before = jnp.asarray(lane[:, None] < lane[None, :], jnp.bfloat16)
    inside = jnp.dot(
        hits16.reshape(kinds * blocks, LANES), before, preferred_element_type=jnp.float32
    ).reshape(kinds, blocks, LANES)
    totals = jnp.sum(hits.astype(jnp.float32), axis=2)
    block = np.arange(blocks)
    base = jnp.dot(
        totals.astype(jnp.bfloat16),
        jnp.asarray(block[:, None] < block[None, :], jnp.bfloat16),
        preferred_element_type=jnp.float32,
    )
    rank = jnp.sum(jnp.where(hits, inside + base[:, :, None], 0.0), axis=0)
    return rank.reshape(count).astype(jnp.int32)


def split16(x, parts):
    pieces = []
    for _ in range(parts):
        piece = x.astype(jnp.bfloat16).astype(jnp.float32)
        pieces.append(piece)
        x = x - piece
    return pieces


def stack16(x, parts):
    pieces = split16(x, parts)
    rows = x.shape[0] * parts
    if rows % 16:
        pieces.append(jnp.zeros((16 - rows % 16, x.shape[1]), jnp.float32))
    return jnp.concatenate(pieces, axis=0).astype(jnp.bfloat16)


def cross_parts(a, b):
    return (
        a[1:2] * b[2:3] - a[2:3] * b[1:2],
        a[2:3] * b[0:1] - a[0:1] * b[2:3],
        a[0:1] * b[1:2] - a[1:2] * b[0:1],
    )


def one_box(b, center_ref, basis_ref, freq_ref, rows_ref, block_ref, wave_ref, lanes_ref, parts_ref):
    count = lanes_ref.shape[2]
    at = pl.multiple_of(b * count, count)
    coef = basis_ref.shape[1]
    cx, cy, cz = center_ref[0, b], center_ref[1, b], center_ref[2, b]
    lanes = jnp.concatenate(
        [rows_ref[pl.ds(at + i * LANES, LANES), :].T[:8] for i in range(count // LANES)], axis=1
    )
    lanes_ref[b] = lanes
    zero = jnp.zeros((1, count), jnp.float32)
    table = jnp.concatenate(
        [lanes[3:6], zero, *cross_parts(lanes[3:6], lanes[0:3]), zero], axis=0
    )
    parts = stack16(table, 3)
    parts_ref[b] = parts
    one = jnp.ones((1, count), jnp.float32)
    offset = jnp.concatenate(
        [lanes[0:1] - cx, lanes[1:2] - cy, lanes[2:3] - cz, one, jnp.zeros((4, count), jnp.float32)],
        axis=0,
    )
    o1, o2, o3 = split16(offset, 3)
    stacked = jnp.concatenate([o3, o2, o2, o1, o1, o1], axis=0).astype(jnp.bfloat16)
    turns = lax.dot_general(
        stacked, freq_ref[...], (((0,), (0,)), ((), ())), preferred_element_type=jnp.float32
    )
    chunk = 32
    highs, lows = [], []
    for c in range(count // chunk):
        wave = cos_turns(turns[c * chunk : (c + 1) * chunk])
        high = wave.astype(jnp.bfloat16)
        highs.append(high)
        lows.append((wave - high.astype(jnp.float32)).astype(jnp.bfloat16))
    high = jnp.concatenate(highs, axis=0)
    low = jnp.concatenate(lows, axis=0)
    wave_ref[pl.ds(at, count), :coef] = high
    wave_ref[pl.ds(at, count), coef:] = low
    sums = jnp.dot(parts, high, preferred_element_type=jnp.float32)
    sums = sums + jnp.dot(parts, low, preferred_element_type=jnp.float32)
    sums = sums[0:8] + sums[8:16] + sums[16:24]
    block_ref[b] = (
        basis_ref[0:1, :] * sums[0:1]
        + basis_ref[1:2, :] * sums[1:2]
        + basis_ref[2:3, :] * sums[2:3]
    )


def group_body(
    idx_ref, center_ref, x_ref, basis_ref, freq_ref,
    rows_ref, block_ref, wave_ref, lanes_ref, parts_ref, scattered,
):
    fill_rows(x_ref, scattered, columns(x_ref))
    zero_rows(rows_ref)
    scatter_rows(idx_ref, scattered, rows_ref, columns(x_ref))

    def step(b, carry):
        one_box(
            b, center_ref, basis_ref, freq_ref, rows_ref, block_ref, wave_ref, lanes_ref, parts_ref
        )
        return carry

    lax.fori_loop(0, block_ref.shape[0], step, 0, unroll=2)


def split_body(x_ref, out_ref):
    f1, f2, f3 = split16(x_ref[...], 3)
    out_ref[...] = jnp.concatenate([f1, f2, f1, f3, f2, f1], axis=0).astype(jnp.bfloat16)


def split_call(x):
    return pl.pallas_call(
        split_body, out_shape=jax.ShapeDtypeStruct((6 * x.shape[0], x.shape[1]), jnp.bfloat16)
    )(x)


def group_call(idx, center, got, basis, freq, boxes, per_box):
    coef = basis.shape[1]
    slots = boxes * per_box
    return pl.pallas_call(
        group_body,
        out_shape=(
            jax.ShapeDtypeStruct((slots + 8, LANES), jnp.float32),
            jax.ShapeDtypeStruct((boxes, 1, coef), jnp.float32),
            jax.ShapeDtypeStruct((slots, 2 * coef), jnp.bfloat16),
            jax.ShapeDtypeStruct((boxes, 8, per_box), jnp.float32),
            jax.ShapeDtypeStruct((boxes, 32, per_box), jnp.bfloat16),
        ),
        in_specs=[pl.BlockSpec(memory_space=pltpu.SMEM)] * 2
        + [pl.BlockSpec(memory_space=pltpu.VMEM)] * 3,
        out_specs=(pl.BlockSpec(memory_space=pltpu.VMEM),) * 5,
        scratch_shapes=[pltpu.VMEM((slots, LANES), jnp.float32)],
        compiler_params=pltpu.CompilerParams(vmem_limit_bytes=VMEM_LIMIT),
    )(idx, center, got, basis, freq)


def one_velocity(b, near_ref, rows_ref, lanes_ref, parts_ref, wave_ref, exp_ref, dir_ref, out_ref):
    per_box = lanes_ref.shape[2]
    here = pl.multiple_of(b * per_box, per_box)
    coef = dir_ref.shape[1]
    near_count = near_ref.shape[1]
    chunk = 32

    def pair_sums(j, target):
        tx, ty, tz = target[0:1], target[1:2], target[2:3]
        pieces = []
        for c in range(per_box // chunk):
            at = pl.multiple_of(j * per_box + c * chunk, chunk)
            s = rows_ref[pl.ds(at, chunk), :]
            dx = tx - s[:, 0:1]
            dy = ty - s[:, 1:2]
            dz = tz - s[:, 2:3]
            r = lax.rsqrt(dx * dx + dy * dy + dz * dz + core_square)
            pieces.append((r * r * r).astype(jnp.bfloat16))
        factor = jnp.concatenate(pieces, axis=0)
        return jnp.dot(parts_ref[j], factor, preferred_element_type=jnp.float32)

    def whole_box(count):
        target = lanes_ref[b]
        weighted = dir_ref[...] * exp_ref[b]
        weighted = jnp.concatenate(
            [weighted, jnp.zeros((LANES - 8, weighted.shape[1]), jnp.float32)], axis=0
        )
        table = jnp.concatenate(split16(weighted.T, 2), axis=1).astype(jnp.bfloat16)
        far = jnp.dot(
            wave_ref[pl.ds(here, per_box), :coef], table, preferred_element_type=jnp.float32
        )
        far = far + jnp.dot(
            wave_ref[pl.ds(here, per_box), coef:], table, preferred_element_type=jnp.float32
        )
        far = far[:, :LANES] + far[:, LANES:]
        sums = pair_sums(near_ref[b, 0], target)
        for v in range(1, count):
            sums = sums + pair_sums(near_ref[b, v], target)
        sums = sums[0:8] + sums[8:16] + sums[16:24]
        near = jnp.concatenate(
            [*cross_parts(sums[0:3], target[0:3]), jnp.zeros((5, per_box), jnp.float32)], axis=0
        ) - jnp.concatenate([sums[4:7], jnp.zeros((5, per_box), jnp.float32)], axis=0)
        total = near * inv_four_pi
        for i in range(per_box // LANES):
            out_ref[pl.ds(here + i * LANES, LANES), :] = far[
                i * LANES : (i + 1) * LANES
            ] + lanes_to_rows(total[:, i * LANES : (i + 1) * LANES])

    held = (near_ref[b, 0] >= 0).astype(jnp.int32)
    for v in range(1, near_count):
        held = held + (near_ref[b, v] >= 0).astype(jnp.int32)
    for count in range(1, near_count + 1):
        pl.when(held == count)(functools.partial(whole_box, count))


def velocity_body(
    idx_ref, near_ref, rows_ref, lanes_ref, parts_ref, wave_ref, exp_ref, dir_ref,
    out_ref, vel, rows,
):
    def step(b, carry):
        one_velocity(
            b, near_ref, rows_ref, lanes_ref, parts_ref, wave_ref, exp_ref, dir_ref, vel
        )
        return carry

    lax.fori_loop(0, lanes_ref.shape[0], step, 0)
    gather_rows(idx_ref, vel, rows, columns(out_ref))
    take_lanes(rows, out_ref, columns(out_ref))


def velocity_call(idx, out_shape, near, rows, lanes, parts, wave, exps, basis_dir):
    slots = wave.shape[0]
    return pl.pallas_call(
        velocity_body,
        out_shape=jax.ShapeDtypeStruct(out_shape, jnp.float32),
        in_specs=[pl.BlockSpec(memory_space=pltpu.SMEM)] * 2
        + [pl.BlockSpec(memory_space=pltpu.VMEM)] * 6,
        out_specs=pl.BlockSpec(memory_space=pltpu.VMEM),
        scratch_shapes=[pltpu.VMEM((slots, LANES), jnp.float32)] * 2,
        compiler_params=pltpu.CompilerParams(vmem_limit_bytes=VMEM_LIMIT),
    )(idx, near, rows, lanes, parts, wave, exps, basis_dir)


def per_device(
    n_age,
    n_box,
    position,
    strength,
    node_box,
    box_order,
    box_center,
    near_list,
    m2l_source,
    m2l_type,
    basis_dir,
    basis_freq,
    basis_phase,
    translation,
):
    groups = n_age * n_box
    node_count = position.shape[1]
    box_local = box_order.shape[0]
    slots_total = 2 * node_count
    per_peer = slots_total // groups
    per_box = slots_total // box_local
    coef = basis_phase.shape[0]
    kind_count = translation.shape[0]
    box_total = groups * box_local

    padded_order = jnp.pad(box_order, (0, LANES - box_local)).reshape(1, LANES)
    all_order = gather_blocks(padded_order, n_age, n_box, 0)[:, :, 0, :box_local].reshape(-1)

    node_slot = jnp.sum(
        jnp.where(
            node_box[None, :] == all_order[:, None],
            jnp.arange(box_total, dtype=jnp.int32)[:, None],
            0,
        ),
        axis=0,
    )
    owner = node_slot // box_local
    label = (node_slot - owner * box_local + 1).astype(jnp.float32)
    send_at = owner * per_peer + ranks(owner, groups)
    fields = jnp.concatenate(
        [position, strength, label[None, :], jnp.zeros((1, node_count), jnp.float32)], axis=0
    )
    payload = permute_call(
        spread_body, send_at, fields, (groups, 8, per_peer), (node_count, slots_total)
    )
    got = exchange(payload, n_box, 2)

    hit_source = (m2l_source[:, :, None] == all_order[None, None, :]).astype(jnp.bfloat16)
    kind_hits = (
        m2l_type[:, :, None] == jnp.arange(kind_count, dtype=jnp.int32)[None, None, :]
    ).astype(jnp.bfloat16)
    list_counts = jnp.einsum(
        "jlt,jlb->tjb", kind_hits, hit_source, preferred_element_type=jnp.float32
    )
    list_counts = list_counts.astype(jnp.bfloat16).reshape(kind_count * box_local, box_total)
    near_local = jnp.sum(
        jnp.where(
            near_list[:, :, None] == box_order[None, None, :],
            jnp.arange(1, box_local + 1, dtype=jnp.int32)[None, None, :],
            0,
        ),
        axis=2,
    ) - 1

    got_label = got[:, 6, :].reshape(-1).astype(jnp.int32) - 1
    live = got_label >= 0
    tile_at = jnp.where(
        live, got_label * per_box + ranks(got_label, box_local), slots_total
    )
    dir_rows = jnp.pad(basis_dir, ((0, 5), (0, 0)))
    waves = jnp.concatenate([basis_freq, basis_phase[None, :]], axis=0) * inv_two_pi
    freq = split_call(jnp.pad(waves, ((0, 4), (0, 0))))
    rows, sums, wave, lanes, parts = group_call(
        tile_at, box_center, got, dir_rows, freq, box_local, per_box
    )
    local_blocks = sums.reshape(box_local, coef).astype(jnp.bfloat16)
    all_blocks = gather_blocks(local_blocks, n_age, n_box, 1).reshape(box_total, coef)
    mixed = jnp.dot(list_counts, all_blocks, preferred_element_type=jnp.float32)
    mixed = mixed.astype(jnp.bfloat16).reshape(kind_count, box_local, coef)
    expansions = jnp.einsum(
        "tjc,tkc->jk", mixed, translation, preferred_element_type=jnp.float32
    )
    back = velocity_call(
        jnp.minimum(tile_at, slots_total - 1),
        (groups, 8, per_peer),
        near_local,
        rows,
        lanes,
        parts,
        wave,
        expansions.reshape(box_local, 1, coef),
        dir_rows,
    )
    returned = exchange(back, n_box, 3)
    out = permute_call(
        collect_body, send_at, returned, (8, node_count), (slots_total, node_count)
    )
    return out[:3]


def solution(mesh):
    n_box = mesh.shape["box"]
    n_age = mesh.shape["age"]
    placed = (
        P(None, AXES),
        P(None, AXES),
        P(AXES),
        P(AXES),
        P(None, AXES),
        P(AXES, None),
        P(AXES, None),
        P(AXES, None),
        P(),
        P(),
        P(),
        P(),
    )
    return jax.shard_map(
        functools.partial(per_device, n_age, n_box),
        mesh=mesh,
        in_specs=placed,
        out_specs=P(None, AXES),
        check_vma=False,
    )
```

```python
import functools

import jax
import jax.numpy as jnp
import numpy as np
from jax import lax
from jax.experimental import pallas as pl
from jax.experimental.pallas import tpu as pltpu
from jax.sharding import PartitionSpec as P

AXES = ("age", "box")
core_square = 0.01
inv_four_pi = 0.07957747154594767
inv_two_pi = 0.15915494309189535
LANES = 128
VMEM_LIMIT = 32 * 1024 * 1024
SMALL_LIMIT = 6 * 1024 * 1024


def cos_coefficients(degree):
    nodes = np.cos(np.pi * (np.arange(64) + 0.5) / 64)
    w = 0.125 * (nodes + 1.0)
    fit = np.polynomial.chebyshev.Chebyshev.fit(
        w, np.cos(2 * np.pi * np.sqrt(w)), degree, domain=[0, 0.25]
    )
    return [float(c) for c in fit.convert(kind=np.polynomial.Polynomial).coef]


COS_COEF = cos_coefficients(6)


def cos_turns(turns):
    v = turns - ((turns + 12582912.0) - 12582912.0)
    w = v * v
    acc = jnp.full_like(w, COS_COEF[-1])
    for c in COS_COEF[-2::-1]:
        acc = acc * w + c
    return acc


def gather_body(n_age, n_box, x_ref, o_ref, send_sem, recv_sem):
    me_age, me_box = lax.axis_index("age"), lax.axis_index("box")
    barrier = pltpu.get_barrier_semaphore()

    def on_box(d):
        return {"age": me_age, "box": lax.rem(me_box + d, n_box)}

    def on_age(d):
        return {"age": lax.rem(me_age + d, n_age), "box": me_box}

    def greet(peer):
        def step(d, carry):
            pl.semaphore_signal(
                barrier, inc=1, device_id=peer(d), device_id_type=pl.DeviceIdType.MESH
            )
            return carry

        return step

    lax.fori_loop(1, n_box, greet(on_box), 0)
    lax.fori_loop(1, n_age, greet(on_age), 0)
    o_ref[me_age, me_box] = x_ref[...]
    pl.semaphore_wait(barrier, n_box - 1 + n_age - 1)

    def along_box(d):
        return pltpu.make_async_remote_copy(
            src_ref=x_ref,
            dst_ref=o_ref.at[me_age, me_box],
            send_sem=send_sem.at[d - 1],
            recv_sem=recv_sem.at[d - 1],
            device_id=on_box(d),
            device_id_type=pl.DeviceIdType.MESH,
        )

    def along_age(d):
        return pltpu.make_async_remote_copy(
            src_ref=o_ref.at[me_age],
            dst_ref=o_ref.at[me_age],
            send_sem=send_sem.at[n_box - 2 + d],
            recv_sem=recv_sem.at[n_box - 2 + d],
            device_id=on_age(d),
            device_id_type=pl.DeviceIdType.MESH,
        )

    def start(copy):
        def step(d, carry):
            copy(d).start()
            return carry

        return step

    def finish(copy):
        def step(d, carry):
            copy(d).wait()
            return carry

        return step

    lax.fori_loop(1, n_box, start(along_box), 0)
    lax.fori_loop(1, n_box, finish(along_box), 0)
    lax.fori_loop(1, n_age, start(along_age), 0)
    lax.fori_loop(1, n_age, finish(along_age), 0)


def gather_blocks(x, n_age, n_box, collective_id):
    copies = n_age + n_box - 2
    return pl.pallas_call(
        functools.partial(gather_body, n_age, n_box),
        out_shape=jax.ShapeDtypeStruct((n_age, n_box) + x.shape, x.dtype),
        in_specs=[pl.BlockSpec(memory_space=pltpu.VMEM)],
        out_specs=pl.BlockSpec(memory_space=pltpu.VMEM),
        scratch_shapes=[
            pltpu.SemaphoreType.DMA((copies,)),
            pltpu.SemaphoreType.DMA((copies,)),
        ],
        compiler_params=pltpu.CompilerParams(
            collective_id=collective_id, has_side_effects=True, vmem_limit_bytes=SMALL_LIMIT
        ),
    )(x)


def exchange_body(n_box, n, x_ref, o_ref, send_sem, recv_sem):
    me = lax.axis_index("age") * n_box + lax.axis_index("box")
    barrier = pltpu.get_barrier_semaphore()

    def place(other):
        return {"age": other // n_box, "box": lax.rem(other, n_box)}

    def greet(d, carry):
        pl.semaphore_signal(
            barrier,
            inc=1,
            device_id=place(lax.rem(me + d, n)),
            device_id_type=pl.DeviceIdType.MESH,
        )
        return carry

    lax.fori_loop(1, n, greet, 0)
    o_ref[me] = x_ref[me]
    pl.semaphore_wait(barrier, n - 1)

    def copy(d):
        other = lax.rem(me + d, n)
        return pltpu.make_async_remote_copy(
            src_ref=x_ref.at[other],
            dst_ref=o_ref.at[me],
            send_sem=send_sem.at[d - 1],
            recv_sem=recv_sem.at[d - 1],
            device_id=place(other),
            device_id_type=pl.DeviceIdType.MESH,
        )

    def send(d, carry):
        copy(d).start()
        return carry

    def finish(d, carry):
        copy(d).wait()
        return carry

    lax.fori_loop(1, n, send, 0)
    lax.fori_loop(1, n, finish, 0)


def exchange(x, n_box, collective_id):
    n = x.shape[0]
    return pl.pallas_call(
        functools.partial(exchange_body, n_box, n),
        out_shape=jax.ShapeDtypeStruct(x.shape, x.dtype),
        in_specs=[pl.BlockSpec(memory_space=pltpu.VMEM)],
        out_specs=pl.BlockSpec(memory_space=pltpu.VMEM),
        scratch_shapes=[
            pltpu.SemaphoreType.DMA((n - 1,)),
            pltpu.SemaphoreType.DMA((n - 1,)),
        ],
        compiler_params=pltpu.CompilerParams(
            collective_id=collective_id, has_side_effects=True, vmem_limit_bytes=SMALL_LIMIT
        ),
    )(x)


def load_lanes(ref, i):
    if len(ref.shape) == 2:
        return ref[:, pl.ds(pl.multiple_of(i * LANES, LANES), LANES)]
    per = ref.shape[2]
    if per >= LANES:
        k = per // LANES
        return ref[i // k, :, pl.ds(pl.multiple_of(lax.rem(i, k) * LANES, LANES), LANES)]
    m = LANES // per
    return jnp.concatenate([ref[i * m + u] for u in range(m)], axis=1)


def store_lanes(ref, i, tile):
    if len(ref.shape) == 2:
        ref[:, pl.ds(pl.multiple_of(i * LANES, LANES), LANES)] = tile
        return
    per = ref.shape[2]
    if per >= LANES:
        k = per // LANES
        ref[i // k, :, pl.ds(pl.multiple_of(lax.rem(i, k) * LANES, LANES), LANES)] = tile
        return
    m = LANES // per
    for u in range(m):
        ref[i * m + u] = tile[:, u * per : (u + 1) * per]


def columns(ref):
    return ref.shape[-1] if len(ref.shape) == 2 else ref.shape[0] * ref.shape[2]


def lanes_to_rows(tile):
    padded = jnp.concatenate([tile, jnp.zeros((LANES - tile.shape[0], LANES), tile.dtype)], axis=0)
    return padded.T


def fill_rows(src_ref, rows_ref, count):
    def step(i, carry):
        at = pl.multiple_of(i * LANES, LANES)
        rows_ref[pl.ds(at, LANES), :] = lanes_to_rows(load_lanes(src_ref, i))
        return carry

    lax.fori_loop(0, count // LANES, step, 0, unroll=8)


def take_lanes(rows_ref, out_ref, count):
    def step(i, carry):
        at = pl.multiple_of(i * LANES, LANES)
        store_lanes(out_ref, i, rows_ref[pl.ds(at, LANES), :].T[:8])
        return carry

    lax.fori_loop(0, count // LANES, step, 0, unroll=8)


def zero_rows(ref):
    def step(i, carry):
        at = pl.multiple_of(i * 8, 8)
        ref[pl.ds(at, 8), :] = jnp.zeros((8, LANES), jnp.float32)
        return carry

    lax.fori_loop(0, ref.shape[0] // 8, step, 0, unroll=8)


def scatter_rows(idx_ref, src_ref, dst_ref, count):
    def step(i, carry):
        at = pl.multiple_of(i * 16, 16)
        block = src_ref[pl.ds(at, 16), :]
        for u in range(16):
            dst_ref[pl.ds(idx_ref[at + u], 1), :] = block[u : u + 1, :]
        return carry

    lax.fori_loop(0, count // 16, step, 0)


def gather_rows(idx_ref, src_ref, dst_ref, count):
    def step(i, carry):
        at = pl.multiple_of(i * 16, 16)
        rows = [src_ref[pl.ds(idx_ref[at + u], 1), :] for u in range(16)]
        dst_ref[pl.ds(at, 16), :] = jnp.concatenate(rows, axis=0)
        return carry

    lax.fori_loop(0, count // 16, step, 0)


def spread_body(idx_ref, x_ref, out_ref, rows, placed):
    fill_rows(x_ref, rows, columns(x_ref))
    zero_rows(placed)
    scatter_rows(idx_ref, rows, placed, columns(x_ref))
    take_lanes(placed, out_ref, columns(out_ref))


def collect_body(idx_ref, x_ref, out_ref, src, rows):
    fill_rows(x_ref, src, columns(x_ref))
    gather_rows(idx_ref, src, rows, columns(out_ref))
    take_lanes(rows, out_ref, columns(out_ref))


def permute_call(body, idx, x, out_shape, scratch_rows):
    return pl.pallas_call(
        body,
        out_shape=jax.ShapeDtypeStruct(out_shape, jnp.float32),
        in_specs=[
            pl.BlockSpec(memory_space=pltpu.SMEM),
            pl.BlockSpec(memory_space=pltpu.VMEM),
        ],
        out_specs=pl.BlockSpec(memory_space=pltpu.VMEM),
        scratch_shapes=[pltpu.VMEM((r, LANES), jnp.float32) for r in scratch_rows],
        compiler_params=pltpu.CompilerParams(vmem_limit_bytes=VMEM_LIMIT),
    )(idx, x)


def ranks(key, kinds):
    count = key.shape[0]
    blocks = count // LANES
    hits = (key[None, :] == jnp.arange(kinds, dtype=jnp.int32)[:, None]).reshape(
        kinds, blocks, LANES
    )
    hits16 = hits.astype(jnp.bfloat16)
    lane = np.arange(LANES)
    before = jnp.asarray(lane[:, None] < lane[None, :], jnp.bfloat16)
    inside = jnp.dot(
        hits16.reshape(kinds * blocks, LANES), before, preferred_element_type=jnp.float32
    ).reshape(kinds, blocks, LANES)
    totals = jnp.sum(hits.astype(jnp.float32), axis=2)
    block = np.arange(blocks)
    base = jnp.dot(
        totals.astype(jnp.bfloat16),
        jnp.asarray(block[:, None] < block[None, :], jnp.bfloat16),
        preferred_element_type=jnp.float32,
    )
    rank = jnp.sum(jnp.where(hits, inside + base[:, :, None], 0.0), axis=0)
    return rank.reshape(count).astype(jnp.int32)


def split16(x, parts):
    pieces = []
    for _ in range(parts):
        piece = x.astype(jnp.bfloat16).astype(jnp.float32)
        pieces.append(piece)
        x = x - piece
    return pieces


def stack16(x, parts):
    pieces = split16(x, parts)
    rows = x.shape[0] * parts
    if rows % 16:
        pieces.append(jnp.zeros((16 - rows % 16, x.shape[1]), jnp.float32))
    return jnp.concatenate(pieces, axis=0).astype(jnp.bfloat16)


def cross_parts(a, b):
    return (
        a[1:2] * b[2:3] - a[2:3] * b[1:2],
        a[2:3] * b[0:1] - a[0:1] * b[2:3],
        a[0:1] * b[1:2] - a[1:2] * b[0:1],
    )


def one_box(b, center_ref, basis_ref, freq_ref, rows_ref, block_ref, wave_ref, lanes_ref, parts_ref):
    count = lanes_ref.shape[2]
    at = pl.multiple_of(b * count, count)
    coef = basis_ref.shape[1]
    cx, cy, cz = center_ref[0, b], center_ref[1, b], center_ref[2, b]
    lanes = jnp.concatenate(
        [rows_ref[pl.ds(at + i * LANES, LANES), :].T[:8] for i in range(count // LANES)], axis=1
    )
    lanes_ref[b] = lanes
    zero = jnp.zeros((1, count), jnp.float32)
    table = jnp.concatenate(
        [lanes[3:6], zero, *cross_parts(lanes[3:6], lanes[0:3]), zero], axis=0
    )
    parts = stack16(table, 3)
    parts_ref[b] = parts
    one = jnp.ones((1, count), jnp.float32)
    offset = jnp.concatenate(
        [lanes[0:1] - cx, lanes[1:2] - cy, lanes[2:3] - cz, one, jnp.zeros((4, count), jnp.float32)],
        axis=0,
    )
    o1, o2, o3 = split16(offset, 3)
    stacked = jnp.concatenate([o3, o2, o2, o1, o1, o1], axis=0).astype(jnp.bfloat16)
    turns = lax.dot_general(
        stacked, freq_ref[...], (((0,), (0,)), ((), ())), preferred_element_type=jnp.float32
    )
    chunk = 32
    highs, lows = [], []
    for c in range(count // chunk):
        wave = cos_turns(turns[c * chunk : (c + 1) * chunk])
        high = wave.astype(jnp.bfloat16)
        highs.append(high)
        lows.append((wave - high.astype(jnp.float32)).astype(jnp.bfloat16))
    high = jnp.concatenate(highs, axis=0)
    low = jnp.concatenate(lows, axis=0)
    wave_ref[pl.ds(at, count), :coef] = high
    wave_ref[pl.ds(at, count), coef:] = low
    sums = jnp.dot(parts, high, preferred_element_type=jnp.float32)
    sums = sums + jnp.dot(parts, low, preferred_element_type=jnp.float32)
    sums = sums[0:8] + sums[8:16] + sums[16:24]
    block_ref[b] = (
        basis_ref[0:1, :] * sums[0:1]
        + basis_ref[1:2, :] * sums[1:2]
        + basis_ref[2:3, :] * sums[2:3]
    )


def group_body(
    idx_ref, center_ref, x_ref, basis_ref, freq_ref,
    rows_ref, block_ref, wave_ref, lanes_ref, parts_ref, scattered,
):
    fill_rows(x_ref, scattered, columns(x_ref))
    zero_rows(rows_ref)
    scatter_rows(idx_ref, scattered, rows_ref, columns(x_ref))

    def step(b, carry):
        one_box(
            b, center_ref, basis_ref, freq_ref, rows_ref, block_ref, wave_ref, lanes_ref, parts_ref
        )
        return carry

    lax.fori_loop(0, block_ref.shape[0], step, 0, unroll=2)


def split_body(x_ref, out_ref):
    f1, f2, f3 = split16(x_ref[...], 3)
    out_ref[...] = jnp.concatenate([f1, f2, f1, f3, f2, f1], axis=0).astype(jnp.bfloat16)


def split_call(x):
    return pl.pallas_call(
        split_body, out_shape=jax.ShapeDtypeStruct((6 * x.shape[0], x.shape[1]), jnp.bfloat16)
    )(x)


def group_call(idx, center, got, basis, freq, boxes, per_box):
    coef = basis.shape[1]
    slots = boxes * per_box
    return pl.pallas_call(
        group_body,
        out_shape=(
            jax.ShapeDtypeStruct((slots + 8, LANES), jnp.float32),
            jax.ShapeDtypeStruct((boxes, 1, coef), jnp.float32),
            jax.ShapeDtypeStruct((slots, 2 * coef), jnp.bfloat16),
            jax.ShapeDtypeStruct((boxes, 8, per_box), jnp.float32),
            jax.ShapeDtypeStruct((boxes, 32, per_box), jnp.bfloat16),
        ),
        in_specs=[pl.BlockSpec(memory_space=pltpu.SMEM)] * 2
        + [pl.BlockSpec(memory_space=pltpu.VMEM)] * 3,
        out_specs=(pl.BlockSpec(memory_space=pltpu.VMEM),) * 5,
        scratch_shapes=[pltpu.VMEM((slots, LANES), jnp.float32)],
        compiler_params=pltpu.CompilerParams(vmem_limit_bytes=VMEM_LIMIT),
    )(idx, center, got, basis, freq)


def one_velocity(b, near_ref, rows_ref, lanes_ref, parts_ref, wave_ref, exp_ref, dir_ref, out_ref):
    per_box = lanes_ref.shape[2]
    here = pl.multiple_of(b * per_box, per_box)
    coef = dir_ref.shape[1]
    near_count = near_ref.shape[1]
    chunk = 32

    def pair_sums(j, target):
        tx, ty, tz = target[0:1], target[1:2], target[2:3]
        pieces = []
        for c in range(per_box // chunk):
            at = pl.multiple_of(j * per_box + c * chunk, chunk)
            s = rows_ref[pl.ds(at, chunk), :]
            dx = tx - s[:, 0:1]
            dy = ty - s[:, 1:2]
            dz = tz - s[:, 2:3]
            r = lax.rsqrt(dx * dx + dy * dy + dz * dz + core_square)
            pieces.append((r * r * r).astype(jnp.bfloat16))
        factor = jnp.concatenate(pieces, axis=0)
        return jnp.dot(parts_ref[j], factor, preferred_element_type=jnp.float32)

    def whole_box(count):
        target = lanes_ref[b]
        table = stack16(dir_ref[...] * exp_ref[b], 2)
        contract = (((1,), (1,)), ((), ()))
        far = lax.dot_general(
            table,
            wave_ref[pl.ds(here, per_box), :coef],
            contract,
            preferred_element_type=jnp.float32,
        )
        far = far + lax.dot_general(
            table,
            wave_ref[pl.ds(here, per_box), coef:],
            contract,
            preferred_element_type=jnp.float32,
        )
        far = far[0:8] + far[8:16]
        sums = pair_sums(near_ref[b, 0], target)
        for v in range(1, count):
            sums = sums + pair_sums(near_ref[b, v], target)
        sums = sums[0:8] + sums[8:16] + sums[16:24]
        near = jnp.concatenate(
            [*cross_parts(sums[0:3], target[0:3]), jnp.zeros((5, per_box), jnp.float32)], axis=0
        ) - jnp.concatenate([sums[4:7], jnp.zeros((5, per_box), jnp.float32)], axis=0)
        total = near * inv_four_pi + far
        for i in range(per_box // LANES):
            out_ref[pl.ds(here + i * LANES, LANES), :] = lanes_to_rows(
                total[:, i * LANES : (i + 1) * LANES]
            )

    held = (near_ref[b, 0] >= 0).astype(jnp.int32)
    for v in range(1, near_count):
        held = held + (near_ref[b, v] >= 0).astype(jnp.int32)
    for count in range(1, near_count + 1):
        pl.when(held == count)(functools.partial(whole_box, count))


def velocity_body(
    idx_ref, near_ref, rows_ref, lanes_ref, parts_ref, wave_ref, exp_ref, dir_ref,
    out_ref, vel, rows,
):
    def step(b, carry):
        one_velocity(
            b, near_ref, rows_ref, lanes_ref, parts_ref, wave_ref, exp_ref, dir_ref, vel
        )
        return carry

    lax.fori_loop(0, lanes_ref.shape[0], step, 0)
    gather_rows(idx_ref, vel, rows, columns(out_ref))
    take_lanes(rows, out_ref, columns(out_ref))


def velocity_call(idx, out_shape, near, rows, lanes, parts, wave, exps, basis_dir):
    slots = wave.shape[0]
    return pl.pallas_call(
        velocity_body,
        out_shape=jax.ShapeDtypeStruct(out_shape, jnp.float32),
        in_specs=[pl.BlockSpec(memory_space=pltpu.SMEM)] * 2
        + [pl.BlockSpec(memory_space=pltpu.VMEM)] * 6,
        out_specs=pl.BlockSpec(memory_space=pltpu.VMEM),
        scratch_shapes=[pltpu.VMEM((slots, LANES), jnp.float32)] * 2,
        compiler_params=pltpu.CompilerParams(vmem_limit_bytes=VMEM_LIMIT),
    )(idx, near, rows, lanes, parts, wave, exps, basis_dir)


def per_device(
    n_age,
    n_box,
    position,
    strength,
    node_box,
    box_order,
    box_center,
    near_list,
    m2l_source,
    m2l_type,
    basis_dir,
    basis_freq,
    basis_phase,
    translation,
):
    groups = n_age * n_box
    node_count = position.shape[1]
    box_local = box_order.shape[0]
    slots_total = 2 * node_count
    per_peer = slots_total // groups
    per_box = slots_total // box_local
    coef = basis_phase.shape[0]
    kind_count = translation.shape[0]
    box_total = groups * box_local

    padded_order = jnp.pad(box_order, (0, LANES - box_local)).reshape(1, LANES)
    all_order = gather_blocks(padded_order, n_age, n_box, 0)[:, :, 0, :box_local].reshape(-1)

    node_slot = jnp.sum(
        jnp.where(
            node_box[None, :] == all_order[:, None],
            jnp.arange(box_total, dtype=jnp.int32)[:, None],
            0,
        ),
        axis=0,
    )
    owner = node_slot // box_local
    label = (node_slot - owner * box_local + 1).astype(jnp.float32)
    send_at = owner * per_peer + ranks(owner, groups)
    fields = jnp.concatenate(
        [position, strength, label[None, :], jnp.zeros((1, node_count), jnp.float32)], axis=0
    )
    payload = permute_call(
        spread_body, send_at, fields, (groups, 8, per_peer), (node_count, slots_total)
    )
    got = exchange(payload, n_box, 2)

    hit_source = (m2l_source[:, :, None] == all_order[None, None, :]).astype(jnp.bfloat16)
    kind_hits = (
        m2l_type[:, :, None] == jnp.arange(kind_count, dtype=jnp.int32)[None, None, :]
    ).astype(jnp.bfloat16)
    list_counts = jnp.einsum(
        "jlt,jlb->tjb", kind_hits, hit_source, preferred_element_type=jnp.float32
    )
    list_counts = list_counts.astype(jnp.bfloat16).reshape(kind_count * box_local, box_total)
    near_local = jnp.sum(
        jnp.where(
            near_list[:, :, None] == box_order[None, None, :],
            jnp.arange(1, box_local + 1, dtype=jnp.int32)[None, None, :],
            0,
        ),
        axis=2,
    ) - 1

    got_label = got[:, 6, :].reshape(-1).astype(jnp.int32) - 1
    live = got_label >= 0
    tile_at = jnp.where(
        live, got_label * per_box + ranks(got_label, box_local), slots_total
    )
    dir_rows = jnp.pad(basis_dir, ((0, 5), (0, 0)))
    waves = jnp.concatenate([basis_freq, basis_phase[None, :]], axis=0) * inv_two_pi
    freq = split_call(jnp.pad(waves, ((0, 4), (0, 0))))
    rows, sums, wave, lanes, parts = group_call(
        tile_at, box_center, got, dir_rows, freq, box_local, per_box
    )
    local_blocks = sums.reshape(box_local, coef).astype(jnp.bfloat16)
    all_blocks = gather_blocks(local_blocks, n_age, n_box, 1).reshape(box_total, coef)
    mixed = jnp.dot(list_counts, all_blocks, preferred_element_type=jnp.float32)
    mixed = mixed.astype(jnp.bfloat16).reshape(kind_count, box_local, coef)
    expansions = jnp.einsum(
        "tjc,tkc->jk", mixed, translation, preferred_element_type=jnp.float32
    )
    back = velocity_call(
        jnp.minimum(tile_at, slots_total - 1),
        (groups, 8, per_peer),
        near_local,
        rows,
        lanes,
        parts,
        wave,
        expansions.reshape(box_local, 1, coef),
        dir_rows,
    )
    returned = exchange(back, n_box, 3)
    out = permute_call(
        collect_body, send_at, returned, (8, node_count), (slots_total, node_count)
    )
    return out[:3]


def solution(mesh):
    n_box = mesh.shape["box"]
    n_age = mesh.shape["age"]
    placed = (
        P(None, AXES),
        P(None, AXES),
        P(AXES),
        P(AXES),
        P(None, AXES),
        P(AXES, None),
        P(AXES, None),
        P(AXES, None),
        P(),
        P(),
        P(),
        P(),
    )
    return jax.shard_map(
        functools.partial(per_device, n_age, n_box),
        mesh=mesh,
        in_specs=placed,
        out_specs=P(None, AXES),
        check_vma=False,
    )
```
